512 devices in a mesh: py: 32 (over x_hi, z), pz: 16 (over y, x_lo, core).
Axes of the slice: x: 4 (x_hi: 2, x_lo: 2; x = x_hi * 2 + x_lo), y: 4, z: 16, core: 2. Of those that a mesh axis runs over, the one named last changes fastest.
Arguments:
- state: bfloat16 [64, 192, 4096], P(None, 'py', 'pz'), may hold values from -6 to 6
- cotangent: bfloat16 [64, 192, 4096], P(None, 'py', 'pz'), may hold values from -6 to 6
- spectral_y: bfloat16 [2, 32, 4096], replicated, may hold values from -0.5 to 0.5
- spectral_z: bfloat16 [2, 32, 4096], replicated, may hold values from -0.5 to 0.5
- w_in: bfloat16 [64, 256], replicated, may hold values from -0.75 to 0.75
- w_out: bfloat16 [256, 64], replicated, may hold values from -0.375 to 0.375
Outputs:
- grad_state: bfloat16 [64, 192, 4096], P(None, 'py', 'pz')
- grad_spectral_y: bfloat16 [2, 32, 4096], replicated
- grad_spectral_z: bfloat16 [2, 32, 4096], replicated
- grad_w_in: bfloat16 [64, 256], replicated
- grad_w_out: bfloat16 [256, 64], replicated
The draws below stay inside these ranges and needn't reach their ends.
All inputs are finite; a program needn't handle non-finite values.
Results may differ from the reference program's by a relative error of at most 0.0076.
Values may be sent and summed in bfloat16 or wider, within the bound.
A program may use at most 64 MiB of HBM per device.

```python
import math
import jax
import jax.numpy as jnp
from jax import lax

CHANNELS = 64
HIDDEN_SIZE = 256
MODES = 32
LEN_Y = 192
LEN_Z = 128
XCELLS = 32


def block_scale(rng, dims, pieces, low, top_value):
    gain = 1.0
    for axis_at, shards_of in pieces:
        draws = jax.random.uniform(jax.random.fold_in(jax.random.fold_in(rng, 6), axis_at), (shards_of,), jnp.float32, low / len(pieces), top_value / len(pieces))
        gain = gain * jnp.repeat(jnp.exp(draws), dims[axis_at] // shards_of).reshape((-1,) + (1,) * (len(dims) - 1 - axis_at))
    return gain


def normal_values(own_key, dims, spread, most, pieces=(), kind=jnp.bfloat16):
    gain = block_scale(own_key, dims, pieces, -0.22, 0.18) if pieces else 1.0
    values = jax.random.normal(own_key, dims, jnp.float32) * spread * gain
    return jnp.minimum(jnp.maximum(values, -most), most).astype(kind)


def setup_inputs(seed: int = 0) -> dict:
    keys = jax.random.split(jax.random.key(seed), 7)
    state = normal_values(keys[0], (CHANNELS, LEN_Y, LEN_Z * XCELLS), 1.0, 6.0, ((1, 32), (2, 16)))
    cotangent = normal_values(keys[1], (CHANNELS, LEN_Y, LEN_Z * XCELLS), 1.0, 6.0, ((1, 32), (2, 16)))
    spectral_y = normal_values(keys[2], (2, MODES, CHANNELS * CHANNELS), (2 * CHANNELS) ** -0.5, 0.5)
    spectral_z = normal_values(keys[3], (2, MODES, CHANNELS * CHANNELS), (2 * CHANNELS) ** -0.5, 0.5)
    w_in = normal_values(keys[4], (CHANNELS, HIDDEN_SIZE), CHANNELS ** -0.5, 0.75)
    w_out = normal_values(keys[5], (HIDDEN_SIZE, CHANNELS), HIDDEN_SIZE ** -0.5, 0.375)
    return dict(state=state, cotangent=cotangent, spectral_y=spectral_y, spectral_z=spectral_z, w_in=w_in, w_out=w_out)


HIGHEST = lax.Precision.HIGHEST

def dft_tables(length, mode_count):
    positions = jnp.arange(length, dtype=jnp.int32)
    frequency = jnp.arange(mode_count, dtype=jnp.int32)
    phase_angle = (jnp.outer(positions, frequency) % length).astype(jnp.float32) * (2.0 * math.pi / length)
    cosine_table = jnp.cos(phase_angle)
    sine_table = jnp.sin(phase_angle)
    weighting = jnp.where(frequency == 0, 1.0, 2.0).astype(jnp.float32) / length
    inverse_re = (cosine_table * weighting[None, :]).T
    inverse_im = -(sine_table * weighting[None, :]).T
    return (cosine_table, -sine_table, inverse_re, inverse_im)

def contract_form(form, first_arg, second_arg):
    return jnp.einsum(form, first_arg, second_arg, precision=HIGHEST)

def pair_product(first_arg, second_arg):
    return lax.dot_general(first_arg, second_arg, (((1,), (1,)), ((), ())), preferred_element_type=jnp.float32)

def branch_forward(values, weights, tables, into_form, back_form, mix_form):
    forward_re, forward_im, inverse_re, inverse_im = tables
    spec_re = contract_form(into_form, values, forward_re)
    spec_im = contract_form(into_form, values, forward_im)
    weight_re = weights[0]
    weight_im = weights[1]
    mixed_re = contract_form(mix_form, spec_re, weight_re) - contract_form(mix_form, spec_im, weight_im)
    mixed_im = contract_form(mix_form, spec_im, weight_re) + contract_form(mix_form, spec_re, weight_im)
    result = contract_form(back_form, mixed_re, inverse_re) + contract_form(back_form, mixed_im, inverse_im)
    return (result, spec_re, spec_im)

def branch_backward(incoming, spec_re, spec_im, weights, tables, into_form, back_form, adjoint_form, outer_form):
    forward_re, forward_im, inverse_re, inverse_im = tables
    grad_re = contract_form(into_form, incoming, inverse_re.T)
    grad_im = contract_form(into_form, incoming, inverse_im.T)
    weight_re = weights[0]
    weight_im = weights[1]
    spec_grad_re = contract_form(adjoint_form, grad_re, weight_re) + contract_form(adjoint_form, grad_im, weight_im)
    spec_grad_im = contract_form(adjoint_form, grad_im, weight_re) - contract_form(adjoint_form, grad_re, weight_im)
    delta_re = contract_form(outer_form, spec_re, grad_re) + contract_form(outer_form, spec_im, grad_im)
    delta_im = contract_form(outer_form, spec_re, grad_im) - contract_form(outer_form, spec_im, grad_re)
    field_grad = contract_form(back_form, spec_grad_re, forward_re.T) + contract_form(back_form, spec_grad_im, forward_im.T)
    return (field_grad, delta_re, delta_im)

def reference(state, cotangent, spectral_y, spectral_z, w_in, w_out):
    field_block = state.reshape(CHANNELS, LEN_Y, LEN_Z, XCELLS)
    cot_field = cotangent.reshape(CHANNELS, LEN_Y, LEN_Z, XCELLS)
    slices = (jnp.moveaxis(field_block, 3, 0), jnp.moveaxis(cot_field, 3, 0))
    weights_y = spectral_y.astype(jnp.float32).reshape(2, MODES, CHANNELS, CHANNELS)
    weights_z = spectral_z.astype(jnp.float32).reshape(2, MODES, CHANNELS, CHANNELS)
    tables_y = dft_tables(LEN_Y, MODES)
    tables_z = dft_tables(LEN_Z, MODES)

    def slice_step(accumulated, slice_pair):
        x_slice, cot_slice = slice_pair
        values = x_slice.astype(jnp.float32)
        result_y, real_y, imag_y = branch_forward(values, weights_y, tables_y, 'cyz,yk->ckz', 'okz,ky->oyz', 'ckz,kco->okz')
        result_z, real_z, imag_z = branch_forward(values, weights_z, tables_z, 'cyz,zk->cky', 'oky,kz->oyz', 'cky,kco->oky')
        branch_y = lax.optimization_barrier(result_y.astype(jnp.bfloat16))
        branch_z = lax.optimization_barrier(result_z.astype(jnp.bfloat16))
        mixed_sum = (branch_y.astype(jnp.float32) + branch_z.astype(jnp.float32)).astype(jnp.bfloat16)
        flattened = mixed_sum.reshape(CHANNELS, LEN_Y * LEN_Z)
        pre_act = jnp.dot(w_in.T, flattened, preferred_element_type=jnp.float32)
        activated, pullback = jax.vjp(jax.nn.gelu, pre_act)
        activated = activated.astype(jnp.bfloat16)
        cot_flat = cot_slice.reshape(CHANNELS, LEN_Y * LEN_Z)
        grad_act = jnp.dot(w_out, cot_flat, preferred_element_type=jnp.float32)
        grad_pre = pullback(grad_act)[0].astype(jnp.bfloat16)
        part_out = pair_product(activated, cot_flat)
        part_in = pair_product(flattened, grad_pre)
        grad_mixed = jnp.dot(w_in, grad_pre, preferred_element_type=jnp.float32).astype(jnp.bfloat16)
        incoming = grad_mixed.reshape(CHANNELS, LEN_Y, LEN_Z).astype(jnp.float32)
        back_y, delta_yr, delta_yi = branch_backward(incoming, real_y, imag_y, weights_y, tables_y, 'cyz,yk->ckz', 'okz,ky->oyz', 'okz,kco->ckz', 'ckz,okz->kco')
        back_z, delta_zr, delta_zi = branch_backward(incoming, real_z, imag_z, weights_z, tables_z, 'cyz,zk->cky', 'oky,kz->oyz', 'oky,kco->cky', 'cky,oky->kco')
        back_y = lax.optimization_barrier(back_y.astype(jnp.bfloat16))
        back_z = lax.optimization_barrier(back_z.astype(jnp.bfloat16))
        summed_grad = (cot_slice.astype(jnp.float32) + back_y.astype(jnp.float32) + back_z.astype(jnp.float32)).astype(jnp.bfloat16)
        updates = (delta_yr, delta_yi, delta_zr, delta_zi, part_in, part_out)
        accumulated = tuple((old + new for old, new in zip(accumulated, updates)))
        return (accumulated, summed_grad)
    spectral_zero = jnp.zeros((MODES, CHANNELS, CHANNELS), jnp.float32)
    start = (spectral_zero, spectral_zero, spectral_zero, spectral_zero, jnp.zeros((CHANNELS, HIDDEN_SIZE), jnp.float32), jnp.zeros((HIDDEN_SIZE, CHANNELS), jnp.float32))
    totals, grads = lax.scan(slice_step, start, slices)
    grad_state = jnp.moveaxis(grads, 0, 3).reshape(CHANNELS, LEN_Y, LEN_Z * XCELLS)
    scale_y = 1.0 / math.sqrt(XCELLS * LEN_Z)
    scale_z = 1.0 / math.sqrt(XCELLS * LEN_Y)
    scale_mlp = 1.0 / math.sqrt(XCELLS * LEN_Y * LEN_Z)
    grad_spectral_y = (jnp.stack([totals[0], totals[1]]) * scale_y).astype(jnp.bfloat16).reshape(2, MODES, CHANNELS * CHANNELS)
    grad_spectral_z = (jnp.stack([totals[2], totals[3]]) * scale_z).astype(jnp.bfloat16).reshape(2, MODES, CHANNELS * CHANNELS)
    grad_w_in = (totals[4] * scale_mlp).astype(jnp.bfloat16)
    grad_w_out = (totals[5] * scale_mlp).astype(jnp.bfloat16)
    return (grad_state, grad_spectral_y, grad_spectral_z, grad_w_in, grad_w_out)
```

```python
import functools
import math

import jax
import jax.numpy as jnp
import numpy as np
from jax import lax
from jax.experimental import pallas as pl
from jax.experimental.pallas import tpu as pltpu
from jax.sharding import PartitionSpec as P

MESH = pl.DeviceIdType.MESH
BF, F32 = jnp.bfloat16, jnp.float32
CH, HID = 64, 256
YL, ZL = 6, 8
LANES = 128


def dot_nn(a, b):
    return lax.dot_general(a, b, (((1,), (0,)), ((), ())), preferred_element_type=F32)


def dot_nt(a, b):
    return lax.dot_general(a, b, (((1,), (1,)), ((), ())), preferred_element_type=F32)


def dot_tn(a, b):
    return lax.dot_general(a, b, (((0,), (0,)), ((), ())), preferred_element_type=F32)


def parts_of(value):
    high = value.astype(BF)
    return high, (value - high.astype(F32)).astype(BF)


def np_parts(table):
    high = table.astype(np.float32).astype(BF)
    low = (table - high.astype(np.float64)).astype(np.float32).astype(BF)
    return high, low


def base_tables(length, modes):
    phase = 2.0 * np.pi * (np.outer(np.arange(modes), np.arange(length)) % length) / length
    weight = np.where(np.arange(modes) == 0, 1.0, 2.0)[:, None] / length
    forward = (np.cos(phase), -np.sin(phase))
    inverse = (weight * np.cos(phase), -weight * np.sin(phase))
    return forward, inverse


def y_tables(pair, spans, modes):
    eye = np.eye(ZL)
    blocks = []
    for table in pair:
        cut = table.reshape(modes, spans, 3, 2)
        for odd in range(2):
            block = np.einsum("ksy,uv->kusyv", cut[..., odd], eye)
            blocks.append(block.reshape(modes * ZL, spans * 3 * ZL))
    return np.concatenate(blocks, 0)


def swap(value):
    return pltpu.roll(value, 64, 1)


def kernel(
    NP,
    NQ,
    xs, cs, my, mz, wi2, wo2, zfh, zfl, zah, zal, zfth, zftl, zath, zatl, ytab_hbm, ytabt_hbm,
    grad_out, mlp_out, spec_out,
    r1, c1, z1, y1s, y1, y2s, y2, z2s, z2, g1, z3, y3s, y3, y4s, y4, z4s, z4, o1,
    rss, rsr, ws, wr, wg, m1s, m1r, m2r,
    pre, gact, actb, gpb, mixb, uz, gz, vz,
    su, sg, dwy, ytab, ytabt, tab_sem, send_sem, recv_sem,
):
    modes = 2 * NQ
    rows = NP * 24
    vrows = modes * ZL
    p, q = lax.axis_index("py"), lax.axis_index("pz")

    barrier = pltpu.get_barrier_semaphore()

    @pl.loop(1, NP)
    def _(i):
        pl.semaphore_signal(barrier, inc=1, device_id=(lax.rem(p + i, NP), q), device_id_type=MESH)

    @pl.loop(1, NQ)
    def _(i):
        pl.semaphore_signal(barrier, inc=1, device_id=(p, lax.rem(q + i, NQ)), device_id_type=MESH)

    pl.semaphore_wait(barrier, NP - 1 + NQ - 1)

    lo = lax.broadcasted_iota(jnp.int32, (1, LANES), 1) < 64
    pending = []

    def send(kind, slot, source, landing, n):
        mine = p if kind == "py" else q

        @pl.loop(1, n)
        def _(i):
            t = lax.rem(mine + i, n)
            pltpu.make_async_remote_copy(
                src_ref=source(t),
                dst_ref=landing.at[mine],
                send_sem=send_sem.at[slot],
                recv_sem=recv_sem.at[slot],
                device_id=(t, q) if kind == "py" else (p, t),
                device_id_type=MESH,
            ).start()

        pending.append((kind, slot, landing, n))

    def drain(kind, slot, landing, n):
        span = landing.at[pl.ds(0, n - 1)]
        return pltpu.make_async_remote_copy(
            src_ref=span,
            dst_ref=span,
            send_sem=send_sem.at[slot],
            recv_sem=recv_sem.at[slot],
            device_id=(p, q),
            device_id_type=MESH,
        )

    def arrived(kind, slot, landing, n):
        drain(kind, slot, landing, n).wait_recv()

    def own(landing, at, value):
        landing[pl.ds(at, 1)] = value

    send("py", 0, lambda t: xs.at[t], r1, NP)
    own(r1, p, xs[pl.ds(p, 1)])
    copies = [
        pltpu.make_async_copy(ytab_hbm, ytab, tab_sem.at[0]),
        pltpu.make_async_copy(ytabt_hbm, ytabt, tab_sem.at[1]),
    ]
    for copy in copies:
        copy.start()
    uz[...] = jnp.zeros_like(uz)
    gz[...] = jnp.zeros_like(gz)
    for copy in copies:
        copy.wait()
    arrived("py", 0, r1, NP)

    def lines(block):
        return block.astype(F32).reshape(rows, LANES).astype(BF)

    def y_analysis(which, field):
        def part(j):
            at = pl.ds(j * vrows, vrows)
            return dot_nn(ytab[which, 0, at], field) + dot_nn(ytab[which, 1, at], field)

        spec = jnp.where(lo, part(0) + swap(part(1)), swap(part(2)) + part(3))
        return spec.astype(BF).reshape(NQ, 2 * ZL, LANES)

    def y_synthesis(which, spec):
        value = spec.astype(F32).reshape(vrows, LANES)
        other = swap(value)
        pieces = [
            jnp.where(lo, value, 0.0), jnp.where(lo, 0.0, other),
            jnp.where(lo, other, 0.0), jnp.where(lo, 0.0, value),
        ]
        stacked = jnp.concatenate(pieces, 0).astype(BF)
        return dot_nn(ytabt[which, 0], stacked) + dot_nn(ytabt[which, 1], stacked)

    def z_analysis(high, low, landing, store):
        both = jnp.concatenate([high[...], low[...]], 1)
        for h in range(2):
            block = landing[:, h].astype(F32)
            for j in range(3):
                cells = block[:, j * ZL:(j + 1) * ZL].reshape(NQ * ZL, LANES).astype(BF)
                spec = dot_nn(both, jnp.concatenate([cells, cells], 0))
                re, im = spec[:modes], spec[modes:]
                at = (h * 3 + j) * 2 * modes
                store[pl.ds(at, modes), :] = jnp.where(lo, re, swap(im))
                store[pl.ds(at + modes, modes), :] = jnp.where(lo, swap(re), im)

    def z_synthesis(high, low, source, sends):
        three = jnp.concatenate([high[...], high[...], low[...]], 1)
        for h in range(2):
            out = []
            for j in range(3):
                at = (h * 3 + j) * 2 * modes
                even, odd = source[pl.ds(at, modes), :], source[pl.ds(at + modes, modes), :]
                spec = jnp.concatenate(
                    [jnp.where(lo, even, swap(odd)), jnp.where(lo, swap(even), odd)], 0
                )
                sh, sl = parts_of(spec)
                cells = dot_nn(three, jnp.concatenate([sh, sl, sh], 0))
                out.append(cells.reshape(NQ, ZL, LANES))
            sends[:, h] = jnp.concatenate(out, 1).astype(BF)

    unroll = min(8, modes)

    def z_mix(source, store, transposed):
        @pl.loop(0, modes // unroll)
        def _(step):
            for j in range(unroll):
                k = step * unroll + j
                high, low = parts_of(source[pl.ds(k, 16, stride=modes), :])
                both = jnp.concatenate([high, low], 0)
                got = dot_nt(both, mz[k]) if transposed else dot_nn(both, mz[k])
                store[pl.ds(k, 16, stride=modes), :] = got[:16] + got[16:]

    def fold(outer):
        top, bottom = outer[:64], swap(outer[64:])
        return top + jnp.where(lo, bottom, -bottom)

    second = (lax.broadcasted_iota(jnp.int32, (vrows, 1), 0) // ZL) % 2 == 1

    def y_mix(landing, dot):
        value = landing[...].reshape(vrows, LANES)
        return jnp.where(second, dot(value, my[1]), dot(value, my[0])).astype(BF).reshape(
            NQ, 2 * ZL, LANES
        )

    send("pz", 1, lambda t: r1.at[pl.ds(2 * t, 2)], z1, NQ)
    send("py", 2, lambda t: cs.at[t], c1, NP)
    own(z1, q, r1[pl.ds(2 * q, 2)].reshape(1, 2, 24, LANES))
    own(c1, p, cs[pl.ds(p, 1)])
    y1s[...] = y_analysis(0, lines(r1[...]))
    send("pz", 3, lambda t: y1s.at[t], y1, NQ)
    own(y1, q, y1s[pl.ds(q, 1)])
    arrived("pz", 3, y1, NQ)
    y2s[...] = y_mix(y1, dot_nn)
    send("pz", 4, lambda t: y2s.at[t], y2, NQ)
    own(y2, q, y2s[pl.ds(q, 1)])
    arrived("pz", 1, z1, NQ)
    z_analysis(zfh, zfl, z1, uz)
    z_mix(uz, vz, False)
    z_synthesis(zath, zatl, vz, z2s)
    send("pz", 5, lambda t: z2s.at[t], z2, NQ)
    own(z2, q, z2s[pl.ds(q, 1)])
    arrived("pz", 4, y2, NQ)
    branch_y = y_synthesis(1, y2[...]).astype(BF)
    arrived("pz", 5, z2, NQ)
    branch_z = z2[...].astype(F32).reshape(rows, LANES)
    mixb[...] = (branch_y.astype(F32) + branch_z).astype(BF)

    pre[...] = dot_nn(mixb[...], wi2[...])
    arrived("py", 2, c1, NP)
    cot = lines(c1[...])
    gact[...] = dot_nn(cot, wo2[...])
    tile = 32 if rows % 32 == 0 else 16

    @pl.loop(0, rows // tile)
    def _(step):
        at = pl.ds(pl.multiple_of(step * tile, tile), tile)
        value = pre[at, :]
        root = math.sqrt(2.0 / math.pi)
        square = value * value
        bend = jnp.tanh(value * (root + (root * 0.044715) * square))
        half = 0.5 + 0.5 * bend
        slope = half + (0.5 * value) * (1.0 - bend * bend) * (root + (3.0 * root * 0.044715) * square)
        actb[at, :] = (value * half).astype(BF)
        gpb[at, :] = (gact[at, :] * slope).astype(BF)

    g1[...] = dot_nt(gpb[...], wi2[...]).reshape(NP, 24, LANES).astype(BF)

    send("pz", 6, lambda t: g1.at[pl.ds(2 * t, 2)], z3, NQ)
    own(z3, q, g1[pl.ds(2 * q, 2)].reshape(1, 2, 24, LANES))
    y3s[...] = y_analysis(1, lines(g1[...]))
    send("pz", 7, lambda t: y3s.at[t], y3, NQ)
    own(y3, q, y3s[pl.ds(q, 1)])

    def diagonal(both):
        return both[:64, :HID] + both[64:, HID:]

    dwi = diagonal(dot_tn(mixb[...], gpb[...]))
    dwo = diagonal(dot_tn(cot, actb[...]))
    share = 256 // NP
    m1s[...] = jnp.concatenate(
        [dwi[:, :LANES], dwi[:, LANES:], dwo[:, :LANES], dwo[:, LANES:]], 0
    ).reshape(NP, share, LANES)
    send("py", 8, lambda t: m1s.at[t], m1r, NP)
    own(m1r, p, m1s[pl.ds(p, 1)])

    arrived("pz", 7, y3, NQ)
    y4s[...] = y_mix(y3, dot_nt)
    send("pz", 9, lambda t: y4s.at[t], y4, NQ)
    own(y4, q, y4s[pl.ds(q, 1)])
    arrived("pz", 6, z3, NQ)
    z_analysis(zah, zal, z3, gz)

    @pl.loop(0, modes // unroll)
    def _(step):
        for j in range(unroll):
            k = step * unroll + j
            uh, ul = parts_of(uz[pl.ds(k, 16, stride=modes), :])
            gh, gl = parts_of(gz[pl.ds(k, 16, stride=modes), :])
            outer = dot_tn(jnp.concatenate([uh, ul, uh], 0), jnp.concatenate([gh, gh, gl], 0))
            rss[step * (unroll // 2) + j // 2, pl.ds((j % 2) * 64, 64), :] = fold(outer).astype(BF)

    send("pz", 10, lambda t: rss.at[t], rsr, NQ)
    own(rsr, q, rss[pl.ds(q, 1)])
    for landing, store in ((y1, su), (y3, sg)):
        value = landing[...].astype(F32)
        for j in range(2):
            at = value[:, j * ZL:(j + 1) * ZL]
            store[j] = at.reshape(NQ * ZL, LANES).astype(BF)

    @pl.loop(0, 2)
    def _(j):
        dwy[j] = fold(dot_tn(su[j], sg[j]))

    z_mix(gz, vz, True)
    z_synthesis(zfth, zftl, vz, z4s)
    send("pz", 11, lambda t: z4s.at[t], z4, NQ)
    own(z4, q, z4s[pl.ds(q, 1)])

    arrived("pz", 9, y4, NQ)
    back_y = y_synthesis(0, y4[...]).astype(BF)
    arrived("pz", 11, z4, NQ)
    back_z = z4[...].astype(F32).reshape(rows, LANES)
    total = cot.astype(F32) + back_y.astype(F32) + back_z
    o1[...] = total.reshape(NP, 24, LANES).astype(BF)
    send("py", 12, lambda t: o1.at[t], grad_out, NP)
    own(grad_out, p, o1[pl.ds(p, 1)])

    arrived("pz", 10, rsr, NQ)
    dwz = jnp.sum(rsr[...].astype(F32), axis=0)
    ws[...] = jnp.concatenate([dwy[0], dwy[1], dwz], 0).reshape(NP, share, LANES)
    send("py", 13, lambda t: ws.at[t], wr, NP)
    own(wr, p, ws[pl.ds(p, 1)])
    arrived("py", 8, m1r, NP)
    own(m2r, q, jnp.sum(m1r[...], axis=0, keepdims=True))
    send("pz", 14, lambda t: m2r.at[q], m2r, NQ)
    arrived("pz", 14, m2r, NQ)
    scale_mlp = 1.0 / math.sqrt(NP * (YL * NP) * (ZL * NQ))
    own(mlp_out, p, jnp.sum(m2r[...], axis=0, keepdims=True) * scale_mlp)
    send("py", 15, lambda t: mlp_out.at[p], mlp_out, NP)
    arrived("py", 13, wr, NP)
    scale_y = 1.0 / math.sqrt(NP * ZL * NQ)
    scale_z = 1.0 / math.sqrt(NP * YL * NP)
    scale = jnp.where(p < NP // 2, scale_y, scale_z)
    own(wg, p, (jnp.sum(wr[...], axis=0, keepdims=True) * scale).astype(BF))
    send("py", 16, lambda t: wg.at[p], wg, NP)
    arrived("py", 16, wg, NP)
    own(spec_out, q, wg[...].reshape(1, NP, share, LANES))
    send("pz", 17, lambda t: wg, spec_out, NQ)
    arrived("py", 12, grad_out, NP)
    arrived("py", 15, mlp_out, NP)
    arrived("pz", 17, spec_out, NQ)
    for item in pending:
        drain(*item).wait_send()


def on_device(NP, NQ, state, cotangent, spectral_y, spectral_z, w_in, w_out):
    modes = 2 * NQ
    rows = NP * 24
    vrows = modes * ZL
    share = 256 // NP

    def to_blocks(field):
        cut = field.reshape(CH, 3, 2, ZL, NP)
        return jnp.transpose(cut, (4, 1, 3, 2, 0)).reshape(NP, 24, LANES)

    def mixing(weights):
        re, im = weights[0], weights[1]
        return jnp.concatenate(
            [jnp.concatenate([re, im], -1), jnp.concatenate([-im, re], -1)], -2
        )

    own_y = lax.dynamic_slice_in_dim(spectral_y, 2 * lax.axis_index("pz"), 2, 1)
    my = mixing(own_y.reshape(2, 2, CH, CH))
    mz = mixing(spectral_z.reshape(2, modes, CH, CH))
    eye = jnp.eye(2, dtype=BF)
    wi2 = jnp.kron(eye, w_in)
    wo2 = jnp.kron(eye, w_out.T)

    forward_y, inverse_y = base_tables(YL * NP, modes)
    forward_z, inverse_z = base_tables(ZL * NQ, modes)
    tabs = [np_parts(y_tables(pair, NP, modes)) for pair in (forward_y, inverse_y)]
    ytab = jnp.asarray(np.stack([np.stack(t) for t in tabs]))
    ytabt = jnp.asarray(np.stack([np.stack([v.T for v in t]) for t in tabs]))
    zf = np_parts(np.concatenate(forward_z, 0))
    za = np_parts(np.concatenate(inverse_z, 0))
    small = [jnp.asarray(v) for v in (*zf, *za, zf[0].T, zf[1].T, za[0].T, za[1].T)]

    vmem = pl.BlockSpec(memory_space=pltpu.VMEM)
    hbm = pl.BlockSpec(memory_space=pl.ANY)
    V = pltpu.VMEM
    field = lambda: V((NP, 24, LANES), BF)
    zbuf = lambda: V((NQ, 2, 24, LANES), BF)
    ybuf = lambda: V((NQ, 2 * ZL, LANES), BF)
    scratch = [
        field(), field(), zbuf(), ybuf(), ybuf(), ybuf(), ybuf(), zbuf(), zbuf(),
        field(), zbuf(), ybuf(), ybuf(), ybuf(), ybuf(), zbuf(), zbuf(), field(),
        V((NQ, 2 * CH, LANES), BF), V((NQ, 2 * CH, LANES), BF),
        V((NP, share, LANES), F32), V((NP, share, LANES), F32), V((NP, share, LANES), BF),
        V((NP, share, LANES), F32), V((NP, share, LANES), F32), V((NQ, share, LANES), F32),
        V((rows, 2 * HID), F32), V((rows, 2 * HID), F32),
        V((rows, 2 * HID), BF), V((rows, 2 * HID), BF), V((rows, LANES), BF),
        V((16 * modes, LANES), F32), V((16 * modes, LANES), F32), V((16 * modes, LANES), F32),
        V((2, NQ * ZL, LANES), BF), V((2, NQ * ZL, LANES), BF), V((2, CH, LANES), F32),
        V((2, 2, 4 * vrows, rows), BF), V((2, 2, rows, 4 * vrows), BF),
        pltpu.SemaphoreType.DMA((2,)),
        pltpu.SemaphoreType.DMA((18,)),
        pltpu.SemaphoreType.DMA((18,)),
    ]
    grad, mlp, spec = pl.pallas_call(
        functools.partial(kernel, NP, NQ),
        out_shape=(
            jax.ShapeDtypeStruct((NP, 24, LANES), BF),
            jax.ShapeDtypeStruct((NP, share, LANES), F32),
            jax.ShapeDtypeStruct((NQ, NP, share, LANES), BF),
        ),
        in_specs=[vmem] * 14 + [hbm] * 2,
        out_specs=(vmem, vmem, vmem),
        scratch_shapes=scratch,
        compiler_params=pltpu.CompilerParams(
            collective_id=0, has_side_effects=True, vmem_limit_bytes=56 * 1024 * 1024
        ),
    )(to_blocks(state), to_blocks(cotangent), my, mz, wi2, wo2, *small, ytab, ytabt)

    grad_state = jnp.transpose(grad.reshape(NP, 3, ZL, 2, CH), (4, 1, 3, 2, 0)).reshape(state.shape)
    spec = spec.reshape(NQ, 2, 2, CH, 2, CH)
    spec = jnp.transpose(spec, (1, 4, 0, 2, 3, 5)).reshape(2, 2, modes, CH * CH)
    mlp = mlp.reshape(2, 2, CH, LANES).astype(BF)
    grad_w_in = jnp.transpose(mlp[0], (1, 0, 2)).reshape(CH, HID)
    grad_w_out = jnp.transpose(mlp[1], (0, 2, 1)).reshape(HID, CH)
    return (grad_state, spec[0], spec[1], grad_w_in, grad_w_out)


def solution(mesh):
    sizes = (mesh.shape["py"], mesh.shape["pz"])
    in_specs = (P(None, "py", "pz"), P(None, "py", "pz"), P(), P(), P(), P())
    out_specs = (P(None, "py", "pz"), P(), P(), P(), P())
    return jax.shard_map(
        functools.partial(on_device, *sizes),
        mesh=mesh,
        in_specs=in_specs,
        out_specs=out_specs,
        check_vma=False,
    )
```

```python
import functools
import math

import jax
import jax.numpy as jnp
import numpy as np
from jax import lax
from jax.experimental import pallas as pl
from jax.experimental.pallas import tpu as pltpu
from jax.sharding import PartitionSpec as P

MESH = pl.DeviceIdType.MESH
BF, F32 = jnp.bfloat16, jnp.float32
CH, HID = 64, 256
YL, ZL = 6, 8
LANES = 128


def dot_nn(a, b):
    return lax.dot_general(a, b, (((1,), (0,)), ((), ())), preferred_element_type=F32)


def dot_nt(a, b):
    return lax.dot_general(a, b, (((1,), (1,)), ((), ())), preferred_element_type=F32)


def dot_tn(a, b):
    return lax.dot_general(a, b, (((0,), (0,)), ((), ())), preferred_element_type=F32)


def parts_of(value):
    high = value.astype(BF)
    return high, (value - high.astype(F32)).astype(BF)


def np_parts(table):
    high = table.astype(np.float32).astype(BF)
    low = (table - high.astype(np.float64)).astype(np.float32).astype(BF)
    return high, low


def base_tables(length, modes):
    phase = 2.0 * np.pi * (np.outer(np.arange(modes), np.arange(length)) % length) / length
    weight = np.where(np.arange(modes) == 0, 1.0, 2.0)[:, None] / length
    forward = (np.cos(phase), -np.sin(phase))
    inverse = (weight * np.cos(phase), -weight * np.sin(phase))
    return forward, inverse


def y_tables(pair, spans, modes):
    cuts = [table.reshape(modes, spans * 3, 2) for table in pair]
    return np.concatenate([cut[..., odd] for cut in cuts for odd in range(2)], 0)


def swap(value):
    return pltpu.roll(value, 64, 1)


def kernel(
    NP,
    NQ,
    state, cotangent, spectral_y, spectral_z, w_in, w_out,
    yf, ya, yft, yat, zfh, zfl, zah, zal, zfth, zftl, zath, zatl,
    grad_state, grad_sy, grad_sz, grad_in, grad_out,
    xs, cs, r1, c1, z1, y1s, y1, y2s, y2, z2s, z2, g1, z3, y3s, y3, y4s, y4, z4s, z4, o1, f1,
    us, ur, gs, gr, ws, wr, wg, parts, gathered, m1s, m1r, m2r, m3r,
    wi2, wo2, my, mz, pre, gact, actb, gpb, mixb, uz, gz, vz, su, sg, dws,
    cells_f, spec_f, turn_f, big_f,
    send_sem, recv_sem, ring_sem,
):
    modes = 2 * NQ
    rows = NP * 24
    vrows = modes * ZL
    share = 256 // NP
    half = NP // 2
    p, q = lax.axis_index("py"), lax.axis_index("pz")
    sibling = q + 1 - 2 * lax.rem(q, 2)

    barrier = pltpu.get_barrier_semaphore()

    @pl.loop(1, NP)
    def _(i):
        pl.semaphore_signal(barrier, inc=1, device_id=(lax.rem(p + i, NP), q), device_id_type=MESH)

    @pl.loop(1, NQ)
    def _(i):
        pl.semaphore_signal(barrier, inc=1, device_id=(p, lax.rem(q + i, NQ)), device_id_type=MESH)

    lo = lax.broadcasted_iota(jnp.int32, (1, LANES), 1) < 64
    pending = []

    def send(kind, slot, source, landing, n, span=(0, half)):
        def start(t, mine, device):
            pltpu.make_async_remote_copy(
                src_ref=source(t),
                dst_ref=landing.at[mine],
                send_sem=send_sem.at[slot],
                recv_sem=recv_sem.at[slot],
                device_id=device,
                device_id_type=MESH,
            ).start()

        if kind == "pz":

            @pl.loop(1, n)
            def _(i):
                t = lax.rem(q + i, n)
                start(t, q, (p, t))

        else:

            @pl.loop(*span)
            def _(i):
                far = half // 2 + (1 - 2 * lax.rem(i, 2)) * ((i + 1) // 2)
                step = lax.rem(p + far + half, half)
                sides = (0, 1) if kind == "py" else (kind,)
                for side in sides:
                    t = step + (lax.rem(p // half + 1 + side, 2) if kind == "py" else side) * half

                    @pl.when(t != p)
                    def _():
                        start(t, p, (t, q))

            if span[1] < half or kind != "py":
                return

        pending.append((slot, landing, n))

    def drain(slot, landing, n):
        span = landing.at[pl.ds(0, n - 1)]
        return pltpu.make_async_remote_copy(
            src_ref=span,
            dst_ref=span,
            send_sem=send_sem.at[slot],
            recv_sem=recv_sem.at[slot],
            device_id=(p, q),
            device_id_type=MESH,
        )

    def arrived(slot, landing, n):
        drain(slot, landing, n).wait_recv()

    def own(landing, at, value):
        landing[pl.ds(at, 1)] = value

    def to_blocks(source, blocks):
        for j in range(3):
            turn_f[...] = jnp.concatenate([source[2 * j], source[2 * j + 1]], 0).astype(F32).T
            for x in range(NP):
                big_f[pl.ds(x * 24 + j * ZL, ZL), :] = turn_f[pl.ds(x, ZL, stride=NP), :]
        blocks[...] = big_f[:rows, :].reshape(NP, 24, LANES).astype(BF)

    def from_blocks(blocks, target):
        big_f[:rows, :] = blocks[...].astype(F32).reshape(rows, LANES)
        for j in range(3):
            cells = [big_f[pl.ds(j * ZL + z, NP, stride=24), :] for z in range(ZL)]
            turned = jnp.concatenate(cells, 0).T.astype(BF)
            target[2 * j] = turned[:64]
            target[2 * j + 1] = turned[64:]

    def mixing(weights):
        @pl.loop(0, 32)
        def _(g):
            at = pl.ds(pl.multiple_of(g * LANES, LANES), LANES)
            re, im = weights[0, :, at].astype(F32), weights[1, :, at].astype(F32)
            re_s, im_s = swap(re), swap(im)
            big_f[pl.ds(2 * g, modes, stride=LANES), :] = jnp.where(lo, re, im_s)
            big_f[pl.ds(2 * g + 1, modes, stride=LANES), :] = jnp.where(lo, re_s, im)
            big_f[pl.ds(64 + 2 * g, modes, stride=LANES), :] = jnp.where(lo, -im, re_s)
            big_f[pl.ds(65 + 2 * g, modes, stride=LANES), :] = jnp.where(lo, -im_s, re)

    to_blocks(state, xs)
    to_blocks(cotangent, cs)
    pl.semaphore_wait(barrier, NP - 1 + NQ - 1)

    send("py", 0, lambda t: xs.at[t], r1, NP)
    own(r1, p, xs[pl.ds(p, 1)])
    own(c1, p, cs[pl.ds(p, 1)])
    mixing(spectral_z)

    @pl.loop(0, modes)
    def _(k):
        mz[k] = big_f[pl.ds(pl.multiple_of(k * LANES, LANES), LANES), :].astype(BF)

    mixing(spectral_y)
    for j in range(2):
        my[j] = big_f[pl.ds(pl.multiple_of((2 * q + j) * LANES, LANES), LANES), :].astype(BF)
    wi2[...] = jnp.zeros_like(wi2)
    wo2[...] = jnp.zeros_like(wo2)
    for j in range(2):
        wi2[j * 64:(j + 1) * 64, j * HID:(j + 1) * HID] = w_in[...]
        wo2[j * 64:(j + 1) * 64, j * HID:(j + 1) * HID] = w_out[...]
    uz[...] = jnp.zeros_like(uz)
    gz[...] = jnp.zeros_like(gz)
    arrived(0, r1, NP)

    def lines(block):
        return block.astype(F32).reshape(rows, LANES)

    def y_analysis(table, field, sends):
        cells_f[...] = lines(field[...])
        for pair in range(ZL // 2):
            two = [cells_f[pl.ds(2 * pair + i, 3 * NP, stride=ZL), :] for i in range(2)]
            both = jnp.concatenate(two, 1).astype(BF)
            spec = dot_nn(table[...], jnp.concatenate([both, both], 0))
            for i in range(2):
                a, b, c, d = (
                    spec[n * modes:(n + 1) * modes, i * LANES:(i + 1) * LANES] for n in range(4)
                )
                spec_f[pl.ds(2 * pair + i, modes, stride=ZL), :] = jnp.where(
                    lo, a + swap(b), swap(c) + d
                )
        sends[...] = spec_f[...].reshape(NQ, 2 * ZL, LANES).astype(BF)

    def y_synthesis(table, spec):
        spec_f[...] = spec[...].astype(F32).reshape(vrows, LANES)
        for pair in range(ZL // 2):
            two = []
            for i in range(2):
                value = spec_f[pl.ds(2 * pair + i, modes, stride=ZL), :]
                other = swap(value)
                two.append(
                    jnp.concatenate(
                        [
                            jnp.where(lo, value, 0.0), jnp.where(lo, 0.0, other),
                            jnp.where(lo, other, 0.0), jnp.where(lo, 0.0, value),
                        ],
                        0,
                    )
                )
            both = jnp.concatenate(two, 1).astype(BF)
            cells = dot_nn(table[...], jnp.concatenate([both, both], 0))
            for i in range(2):
                cells_f[pl.ds(2 * pair + i, 3 * NP, stride=ZL), :] = cells[
                    :, i * LANES:(i + 1) * LANES
                ]

    def z_analysis(high, low, landing, store):
        both = jnp.concatenate([high[...], low[...]], 1)
        for h in range(2):
            block = landing[:, h].astype(F32)
            for j in range(3):
                cells = block[:, j * ZL:(j + 1) * ZL].reshape(NQ * ZL, LANES).astype(BF)
                spec = dot_nn(both, jnp.concatenate([cells, cells], 0))
                re, im = spec[:modes], spec[modes:]
                at = (h * 3 + j) * 2 * modes
                store[pl.ds(at, modes), :] = jnp.where(lo, re, swap(im))
                store[pl.ds(at + modes, modes), :] = jnp.where(lo, swap(re), im)

    def z_synthesis(high, low, source, sends):
        three = jnp.concatenate([high[...], high[...], low[...]], 1)
        for h in range(2):
            out = []
            for j in range(3):
                at = (h * 3 + j) * 2 * modes
                even, odd = source[pl.ds(at, modes), :], source[pl.ds(at + modes, modes), :]
                spec = jnp.concatenate(
                    [jnp.where(lo, even, swap(odd)), jnp.where(lo, swap(even), odd)], 0
                )
                sh, sl = parts_of(spec)
                cells = dot_nn(three, jnp.concatenate([sh, sl, sh], 0))
                out.append(cells.reshape(NQ, ZL, LANES))
            sends[:, h] = jnp.concatenate(out, 1).astype(BF)

    unroll = min(8, modes)

    def z_split(source, sends):
        @pl.loop(0, modes // unroll)
        def _(step):
            for j in range(unroll):
                k = step * unroll + j
                sends[k] = source[pl.ds(k, 16, stride=modes), :].astype(BF)

    def z_mix(source, store, transposed):
        @pl.loop(0, modes // unroll)
        def _(step):
            for j in range(unroll):
                k = step * unroll + j
                high, low = parts_of(source[pl.ds(k, 16, stride=modes), :])
                both = jnp.concatenate([high, low], 0)
                got = dot_nt(both, mz[k]) if transposed else dot_nn(both, mz[k])
                store[pl.ds(k, 16, stride=modes), :] = got[:16] + got[16:]

    def fold(outer):
        top, bottom = outer[:64], swap(outer[64:])
        return top + jnp.where(lo, bottom, -bottom)

    second = (lax.broadcasted_iota(jnp.int32, (vrows, 1), 0) // ZL) % 2 == 1

    def y_mix(landing, dot):
        value = landing[...].reshape(vrows, LANES)
        return jnp.where(second, dot(value, my[1]), dot(value, my[0])).astype(BF).reshape(
            NQ, 2 * ZL, LANES
        )

    send("pz", 1, lambda t: r1.at[pl.ds(2 * t, 2)], z1, NQ)
    own(z1, q, r1[pl.ds(2 * q, 2)].reshape(1, 2, 24, LANES))
    y_analysis(yf, r1, y1s)
    send("pz", 3, lambda t: y1s.at[t], y1, NQ)
    send("py", 2, lambda t: cs.at[t], c1, NP)
    own(y1, q, y1s[pl.ds(q, 1)])
    arrived(1, z1, NQ)
    z_analysis(zfh, zfl, z1, uz)
    z_mix(uz, vz, False)
    z_synthesis(zath, zatl, vz, z2s)
    send("pz", 5, lambda t: z2s.at[t], z2, NQ)
    own(z2, q, z2s[pl.ds(q, 1)])
    arrived(3, y1, NQ)
    y2s[...] = y_mix(y1, dot_nn)
    send("pz", 4, lambda t: y2s.at[t], y2, NQ)
    own(y2, q, y2s[pl.ds(q, 1)])
    z_split(uz, us)
    send("pz", 17, lambda t: us.at[pl.ds(2 * t, 2)], ur, NQ)
    own(ur, q, us[pl.ds(2 * q, 2)].reshape(1, 2, 16, LANES))
    arrived(4, y2, NQ)
    y_synthesis(yat, y2)
    arrived(5, z2, NQ)
    mixb[...] = (cells_f[...].astype(BF).astype(F32) + lines(z2[...])).astype(BF)

    pre[...] = dot_nn(mixb[...], wi2[...])
    arrived(2, c1, NP)
    cot = lines(c1[...]).astype(BF)
    gact[...] = dot_nn(cot, wo2[...])
    tile = 32 if rows % 32 == 0 else 16

    @pl.loop(0, rows // tile)
    def _(step):
        at = pl.ds(pl.multiple_of(step * tile, tile), tile)
        value = pre[at, :]
        root = math.sqrt(2.0 / math.pi)
        square = value * value
        bend = jnp.tanh(value * (root + (root * 0.044715) * square))
        rise = 0.5 + 0.5 * bend
        slope = rise + (0.5 * value) * (1.0 - bend * bend) * (root + (3.0 * root * 0.044715) * square)
        actb[at, :] = (value * rise).astype(BF)
        gpb[at, :] = (gact[at, :] * slope).astype(BF)

    g1[...] = dot_nt(gpb[...], wi2[...]).reshape(NP, 24, LANES).astype(BF)

    send("pz", 6, lambda t: g1.at[pl.ds(2 * t, 2)], z3, NQ)
    own(z3, q, g1[pl.ds(2 * q, 2)].reshape(1, 2, 24, LANES))
    y_analysis(ya, g1, y3s)
    send("pz", 7, lambda t: y3s.at[t], y3, NQ)
    own(y3, q, y3s[pl.ds(q, 1)])

    def diagonal(both):
        return both[:64, :HID] + both[64:, HID:]

    dwi = diagonal(dot_tn(mixb[...], gpb[...]))
    dwo = diagonal(dot_tn(cot, actb[...]))
    m1s[...] = jnp.concatenate(
        [dwi[:, :LANES], dwi[:, LANES:], dwo[:, :LANES], dwo[:, LANES:]], 0
    ).reshape(NP, share, LANES).astype(BF)
    send("py", 8, lambda t: m1s.at[t], m1r, NP)
    own(m1r, p, m1s[pl.ds(p, 1)])

    arrived(6, z3, NQ)
    z_analysis(zah, zal, z3, gz)
    z_split(gz, gs)
    send("pz", 10, lambda t: gs.at[pl.ds(2 * t, 2)], gr, NQ)
    own(gr, q, gs[pl.ds(2 * q, 2)].reshape(1, 2, 16, LANES))
    arrived(7, y3, NQ)
    y4s[...] = y_mix(y3, dot_nt)
    send("pz", 9, lambda t: y4s.at[t], y4, NQ)
    own(y4, q, y4s[pl.ds(q, 1)])

    for landing, store in ((y1, su), (y3, sg)):
        value = landing[...].astype(F32)
        for j in range(2):
            at = value[:, j * ZL:(j + 1) * ZL]
            store[j] = at.reshape(NQ * ZL, LANES).astype(BF)

    @pl.loop(0, 2)
    def _(j):
        dws[j] = fold(dot_tn(su[j], sg[j]))

    def scatter(branch, slot):
        ws[branch] = dws[2 * branch:2 * branch + 2].reshape(half, share, LANES).astype(BF)
        send(branch, slot, lambda t: ws.at[branch, t - branch * half], wr, NP)

        @pl.when(p // half == branch)
        def _():
            own(wr, p, ws[branch, pl.ds(p - branch * half, 1)])

    def gather(branch, slot, into, scale):
        @pl.when(p // half == branch)
        def _():
            arrived(slot, wr, NP)
            wg[...] = (jnp.sum(wr[...].astype(F32), axis=0) * scale).astype(BF)
            own(parts.at[branch], p - branch * half, wg[...].reshape(1, share, LANES))

            @pl.loop(0, half)
            def _(i):
                far = half // 2 + (1 - 2 * lax.rem(i, 2)) * ((i + 1) // 2)
                step = lax.rem(p + far + half, half)
                for side in (0, 1):
                    t = step + lax.rem(branch + 1 + side, 2) * half

                    @pl.when(t != p)
                    def _():
                        pltpu.make_async_remote_copy(
                            src_ref=wg,
                            dst_ref=parts.at[branch, p - branch * half],
                            send_sem=send_sem.at[into],
                            recv_sem=recv_sem.at[into],
                            device_id=(t, q),
                            device_id_type=MESH,
                        ).start()

    def settle(branch, slot, into):
        @pl.when(p // half == branch)
        def _():
            drain(slot, ws.at[branch], half).wait_send()
            drain(into, wr, NP).wait_send()

        @pl.when(p // half != branch)
        def _():
            drain(slot, ws.at[branch], half + 1).wait_send()

    scatter(0, 13)
    z_mix(gz, vz, True)
    z_synthesis(zfth, zftl, vz, z4s)
    send("pz", 11, lambda t: z4s.at[t], z4, NQ)
    own(z4, q, z4s[pl.ds(q, 1)])
    arrived(17, ur, NQ)
    arrived(10, gr, NQ)

    @pl.loop(0, 2)
    def _(j):
        dws[2 + j] = fold(
            dot_tn(ur[:, j].reshape(NQ * 16, LANES), gr[:, j].reshape(NQ * 16, LANES))
        )

    scatter(1, 15)
    arrived(8, m1r, NP)
    own(m2r, q, jnp.sum(m1r[...].astype(F32), axis=0, keepdims=True))
    send("pz", 14, lambda t: m2r.at[q], m2r, NQ)

    arrived(9, y4, NQ)
    y_synthesis(yft, y4)
    arrived(11, z4, NQ)
    total = lines(c1[...]) + cells_f[...].astype(BF).astype(F32) + lines(z4[...])
    o1[...] = total.reshape(NP, 24, LANES).astype(BF)
    scale_y = 1.0 / math.sqrt(NP * ZL * NQ)
    scale_z = 1.0 / math.sqrt(NP * YL * NP)
    scale_mlp = 1.0 / math.sqrt(NP * (YL * NP) * (ZL * NQ))
    gather(0, 13, 16, scale_y)
    send("py", 12, lambda t: o1.at[t], f1, NP, (0, half // 2))
    own(f1, p, o1[pl.ds(p, 1)])
    gather(1, 15, 18, scale_z)
    send("py", 12, lambda t: o1.at[t], f1, NP, (half // 2, half))
    arrived(14, m2r, NQ)
    own(m3r, p, (jnp.sum(m2r[...], axis=0, keepdims=True) * scale_mlp).astype(BF))
    send("py", 19, lambda t: m3r.at[p], m3r, NP)

    def ring(branch, slot, device):
        at = gathered.at[branch, slot]
        return pltpu.make_async_remote_copy(
            src_ref=at,
            dst_ref=at,
            send_sem=send_sem.at[20 + branch],
            recv_sem=ring_sem.at[branch, slot],
            device_id=(p, device),
            device_id_type=MESH,
        )

    def ring_start(branch, into):
        @pl.when(p // half == branch)
        def _():
            drain(into, parts.at[branch], half).wait_recv()

        @pl.when(p // half != branch)
        def _():
            drain(into, parts.at[branch], half + 1).wait_recv()

        own(gathered.at[branch], q, parts[branch].reshape(1, half, share, LANES))

        @pl.loop(1, NQ // 2)
        def _(j):
            ring(branch, q, lax.rem(q + 2 * j, NQ)).start()

        ring(branch, q, sibling).start()

    def ring_pass(branch):
        @pl.loop(1, NQ // 2)
        def _(j):
            slot = lax.rem(q + 2 * j, NQ)
            ring(branch, slot, sibling).wait_recv()
            ring(branch, slot, sibling).start()

    def ring_end(branch, target):
        @pl.loop(0, NQ // 2)
        def _(j):
            ring(branch, lax.rem(sibling + 2 * j, NQ), sibling).wait_recv()

        big_f[:modes * CH, :] = gathered[branch].astype(F32).reshape(modes * CH, LANES)

        @pl.loop(0, 32)
        def _(g):
            at = pl.ds(pl.multiple_of(g * LANES, LANES), LANES)
            even = big_f[pl.ds(2 * g, modes, stride=CH), :]
            odd = big_f[pl.ds(2 * g + 1, modes, stride=CH), :]
            target[0, :, at] = jnp.where(lo, even, swap(odd)).astype(BF)
            target[1, :, at] = jnp.where(lo, swap(even), odd).astype(BF)

    ring_start(0, 16)
    ring_pass(0)
    ring_start(1, 18)
    ring_end(0, grad_sy)
    arrived(12, f1, NP)
    from_blocks(f1, grad_state)
    ring_pass(1)
    arrived(19, m3r, NP)
    small = m3r[...].reshape(256, LANES)
    grad_in[...] = jnp.concatenate([small[:64], small[64:128]], 1)
    grad_out[...] = jnp.concatenate([small[128:192], small[192:]], 1)
    ring_end(1, grad_sz)

    for item in pending:
        drain(*item).wait_send()
    settle(0, 13, 16)
    settle(1, 15, 18)
    for branch in range(2):
        drain(20 + branch, gathered.at[branch], NQ).wait_send()


def on_device(NP, NQ, state, cotangent, spectral_y, spectral_z, w_in, w_out):
    modes = 2 * NQ
    rows = NP * 24
    vrows = modes * ZL
    share = 256 // NP

    forward_y, inverse_y = base_tables(YL * NP, modes)
    forward_z, inverse_z = base_tables(ZL * NQ, modes)
    yf = np_parts(y_tables(forward_y, NP, modes))
    ya = np_parts(y_tables(inverse_y, NP, modes))
    zf = np_parts(np.concatenate(forward_z, 0))
    za = np_parts(np.concatenate(inverse_z, 0))
    tables = [np.concatenate(yf, 1), np.concatenate(ya, 1)]
    tables += [np.concatenate([v.T for v in yf], 1), np.concatenate([v.T for v in ya], 1)]
    tables += [*zf, *za, zf[0].T, zf[1].T, za[0].T, za[1].T]

    vmem = pl.BlockSpec(memory_space=pltpu.VMEM)
    V = pltpu.VMEM
    field = lambda: V((NP, 24, LANES), BF)
    zbuf = lambda: V((NQ, 2, 24, LANES), BF)
    ybuf = lambda: V((NQ, 2 * ZL, LANES), BF)
    pack = lambda kind: V((NP, share, LANES), kind)
    scratch = [
        field(), field(), field(), field(), zbuf(), ybuf(), ybuf(), ybuf(), ybuf(), zbuf(), zbuf(),
        field(), zbuf(), ybuf(), ybuf(), ybuf(), ybuf(), zbuf(), zbuf(), field(), field(),
        V((modes, 16, LANES), BF), V((NQ, 2, 16, LANES), BF),
        V((modes, 16, LANES), BF), V((NQ, 2, 16, LANES), BF),
        V((2, NP // 2, share, LANES), BF), pack(BF), V((share, LANES), BF),
        V((2, NP // 2, share, LANES), BF), V((2, NQ, NP // 2, share, LANES), BF),
        pack(BF), pack(BF), V((NQ, share, LANES), F32), pack(BF),
        V((LANES, 2 * HID), BF), V((LANES, 2 * HID), BF),
        V((2, LANES, LANES), BF), V((modes, LANES, LANES), BF),
        V((rows, 2 * HID), F32), V((rows, 2 * HID), F32),
        V((rows, 2 * HID), BF), V((rows, 2 * HID), BF), V((rows, LANES), BF),
        V((16 * modes, LANES), F32), V((16 * modes, LANES), F32), V((16 * modes, LANES), F32),
        V((2, NQ * ZL, LANES), BF), V((2, NQ * ZL, LANES), BF), V((4, CH, LANES), F32),
        V((rows, LANES), F32), V((vrows, LANES), F32),
        V((ZL * NP, LANES), F32),
        V((max(modes * LANES, rows), LANES), F32),
        pltpu.SemaphoreType.DMA((22,)),
        pltpu.SemaphoreType.DMA((22,)),
        pltpu.SemaphoreType.DMA((2, NQ)),
    ]
    state, cotangent = (jnp.transpose(v, (1, 0, 2)) for v in (state, cotangent))
    shape = lambda like: jax.ShapeDtypeStruct(like.shape, BF)
    grad, grad_sy, grad_sz, grad_in, grad_out = pl.pallas_call(
        functools.partial(kernel, NP, NQ),
        out_shape=tuple(shape(v) for v in (state, spectral_y, spectral_z, w_in, w_in)),
        in_specs=[vmem] * (6 + len(tables)),
        out_specs=(vmem,) * 5,
        scratch_shapes=scratch,
        compiler_params=pltpu.CompilerParams(
            collective_id=0, has_side_effects=True, vmem_limit_bytes=56 * 1024 * 1024
        ),
    )(state, cotangent, spectral_y, spectral_z, w_in, w_out.T, *[jnp.asarray(t) for t in tables])
    return (jnp.transpose(grad, (1, 0, 2)), grad_sy, grad_sz, grad_in, grad_out.T)


def solution(mesh):
    sizes = (mesh.shape["py"], mesh.shape["pz"])
    in_specs = (P(None, "py", "pz"), P(None, "py", "pz"), P(), P(), P(), P())
    out_specs = (P(None, "py", "pz"), P(), P(), P(), P())
    return jax.shard_map(
        functools.partial(on_device, *sizes),
        mesh=mesh,
        in_specs=in_specs,
        out_specs=out_specs,
        check_vma=False,
    )
```

```python
import functools
import math

import jax
import jax.numpy as jnp
import numpy as np
from jax import lax
from jax.experimental import pallas as pl
from jax.experimental.pallas import tpu as pltpu
from jax.sharding import PartitionSpec as P

MESH = pl.DeviceIdType.MESH
BF, F32 = jnp.bfloat16, jnp.float32
CH, HID = 64, 256
YL, ZL = 6, 8
LANES = 128


def dot_nn(a, b):
    return lax.dot_general(a, b, (((1,), (0,)), ((), ())), preferred_element_type=F32)


def dot_nt(a, b):
    return lax.dot_general(a, b, (((1,), (1,)), ((), ())), preferred_element_type=F32)


def dot_tn(a, b):
    return lax.dot_general(a, b, (((0,), (0,)), ((), ())), preferred_element_type=F32)


def parts_of(value):
    high = value.astype(BF)
    return high, (value - high.astype(F32)).astype(BF)


def np_parts(table):
    high = table.astype(np.float32).astype(BF)
    low = (table - high.astype(np.float64)).astype(np.float32).astype(BF)
    return high, low


def base_tables(length, modes):
    phase = 2.0 * np.pi * (np.outer(np.arange(modes), np.arange(length)) % length) / length
    weight = np.where(np.arange(modes) == 0, 1.0, 2.0)[:, None] / length
    forward = (np.cos(phase), -np.sin(phase))
    inverse = (weight * np.cos(phase), -weight * np.sin(phase))
    return forward, inverse


def y_tables(pair, spans, modes):
    cuts = [table.reshape(modes, spans * 3, 2) for table in pair]
    return np.concatenate([cut[..., odd] for cut in cuts for odd in range(2)], 0)


def swap(value):
    return pltpu.roll(value, 64, 1)


def kernel(
    NP,
    NQ,
    state_in, cot_in, spectral_y, spectral_z, w_in_hbm, w_out_hbm, ytab_hbm, ytabt_hbm, ztab_hbm, ztabt_hbm,
    grad_state, grad_sy, grad_sz, grad_in, grad_out,
    xs, cs, r1, c1, z1, y1s, y1, y2s, y2, z2s, z2, g1, z3, y3s, y3, y4s, y4, z4s, z4, o1, f1,
    us, ur, gs, gr, ws, wr, wg, parts, m1s, m1r, m2r, m3r,
    wi2, wo2, my, mz, pre, gact, actb, gpb, mixb, cotb, uz, gz, vz, su, sg, dws,
    cells_f, spec_f, turn_f, big_f,
    weights_f, state, cotangent, w_in, w_out, ytab, ytabt, ztab, ztabt,
    send_sem, recv_sem, ring_sem, fetch_sem, state_sem,
):
    modes = 2 * NQ
    rows = NP * 24
    vrows = modes * ZL
    share = 256 // NP
    half = NP // 2
    p, q = lax.axis_index("py"), lax.axis_index("pz")
    sibling = q + 1 - 2 * lax.rem(q, 2)

    barrier = pltpu.get_barrier_semaphore()

    @pl.loop(1, NP)
    def _(i):
        pl.semaphore_signal(barrier, inc=1, device_id=(lax.rem(p + i, NP), q), device_id_type=MESH)

    @pl.loop(1, NQ)
    def _(i):
        pl.semaphore_signal(barrier, inc=1, device_id=(p, lax.rem(q + i, NQ)), device_id_type=MESH)

    lo = lax.broadcasted_iota(jnp.int32, (1, LANES), 1) < 64
    pending = []

    def send(kind, slot, source, landing, n, span=(0, half), each=None):
        def start(t, mine, device):
            pltpu.make_async_remote_copy(
                src_ref=source(t),
                dst_ref=landing.at[mine],
                send_sem=send_sem.at[slot],
                recv_sem=recv_sem.at[slot] if each is None else each.at[mine],
                device_id=device,
                device_id_type=MESH,
            ).start()

        if kind == "pz":

            @pl.loop(1, n)
            def _(i):
                t = lax.rem(q + i, n)
                start(t, q, (p, t))

        else:

            @pl.loop(*span)
            def _(i):
                far = half // 2 + (1 - 2 * lax.rem(i, 2)) * ((i + 1) // 2)
                step = lax.rem(p + far + half, half)
                sides = (0, 1) if kind == "py" else (kind,)
                for side in sides:
                    t = step + (lax.rem(p // half + 1 + side, 2) if kind == "py" else side) * half

                    @pl.when(t != p)
                    def _():
                        start(t, p, (t, q))

            if span[1] < half or kind != "py":
                return

        pending.append((slot, landing, n))

    def drain(slot, landing, n):
        span = landing.at[pl.ds(0, n - 1)]
        return pltpu.make_async_remote_copy(
            src_ref=span,
            dst_ref=span,
            send_sem=send_sem.at[slot],
            recv_sem=recv_sem.at[slot],
            device_id=(p, q),
            device_id_type=MESH,
        )

    def arrived(slot, landing, n):
        drain(slot, landing, n).wait_recv()

    def own(landing, at, value):
        landing[pl.ds(at, 1)] = value

    def to_blocks(source, blocks):
        for j in range(3):
            turn_f[...] = jnp.concatenate([source[2 * j], source[2 * j + 1]], 0).astype(F32).T
            for x in range(NP):
                big_f[pl.ds(x * 24 + j * ZL, ZL), :] = turn_f[pl.ds(x, ZL, stride=NP), :]
        blocks[...] = big_f[:rows, :].reshape(NP, 24, LANES).astype(BF)

    def from_blocks(blocks, target):
        big_f[:rows, :] = blocks[...].astype(F32).reshape(rows, LANES)
        for j in range(3):
            cells = [big_f[pl.ds(j * ZL + z, NP, stride=24), :] for z in range(ZL)]
            turned = jnp.concatenate(cells, 0).T.astype(BF)
            target[2 * j] = turned[:64]
            target[2 * j + 1] = turned[64:]

    def mixing(weights):
        @pl.loop(0, 8)
        def _(step):
            for n in range(4):
                g = step * 4 + n
                at = pl.ds(pl.multiple_of(g * LANES, LANES), LANES)
                re, im = weights[0, :, at].astype(F32), weights[1, :, at].astype(F32)
                re_s, im_s = swap(re), swap(im)
                big_f[pl.ds(2 * g, modes, stride=LANES), :] = jnp.where(lo, re, im_s)
                big_f[pl.ds(2 * g + 1, modes, stride=LANES), :] = jnp.where(lo, re_s, im)
                big_f[pl.ds(64 + 2 * g, modes, stride=LANES), :] = jnp.where(lo, -im, re_s)
                big_f[pl.ds(65 + 2 * g, modes, stride=LANES), :] = jnp.where(lo, -im_s, re)

    fetches = [
        pltpu.make_async_copy(source, target, fetch_sem.at[n])
        for n, (source, target) in enumerate(
            [
                (state_in, state), (cot_in, cotangent),
                (spectral_z, weights_f.at[0]), (spectral_y, weights_f.at[1]),
                (w_in_hbm, w_in), (w_out_hbm, w_out),
                (ytab_hbm, ytab), (ytabt_hbm, ytabt), (ztab_hbm, ztab), (ztabt_hbm, ztabt),
            ]
        )
    ]
    for fetch in fetches:
        fetch.start()
    fetches[0].wait()
    to_blocks(state, xs)
    pl.semaphore_wait(barrier, NP - 1 + NQ - 1)

    send("py", 0, lambda t: xs.at[t], r1, NP, each=state_sem)
    own(r1, p, xs[pl.ds(p, 1)])
    fetches[1].wait()
    to_blocks(cotangent, cs)
    for fetch in fetches[2:]:
        fetch.wait()
    mixing(weights_f.at[0])

    @pl.loop(0, modes)
    def _(k):
        mz[k] = big_f[pl.ds(pl.multiple_of(k * LANES, LANES), LANES), :].astype(BF)

    mixing(weights_f.at[1])
    for j in range(2):
        my[j] = big_f[pl.ds(pl.multiple_of((2 * q + j) * LANES, LANES), LANES), :].astype(BF)
    wi2[...] = jnp.zeros_like(wi2)
    wo2[...] = jnp.zeros_like(wo2)
    for j in range(2):
        wi2[j * 64:(j + 1) * 64, j * HID:(j + 1) * HID] = w_in[...]
        wo2[j * 64:(j + 1) * 64, j * HID:(j + 1) * HID] = w_out[...]
    uz[...] = jnp.zeros_like(uz)
    gz[...] = jnp.zeros_like(gz)
    def lines(block):
        return block.astype(F32).reshape(rows, LANES)

    def y_analysis(table, field, sends):
        cells_f[...] = lines(field[...])
        for pair in range(ZL // 2):
            two = [cells_f[pl.ds(2 * pair + i, 3 * NP, stride=ZL), :] for i in range(2)]
            both = jnp.concatenate(two, 1).astype(BF)
            spec = dot_nn(table[...], jnp.concatenate([both, both], 0))
            for i in range(2):
                a, b, c, d = (
                    spec[n * modes:(n + 1) * modes, i * LANES:(i + 1) * LANES] for n in range(4)
                )
                spec_f[pl.ds(2 * pair + i, modes, stride=ZL), :] = jnp.where(
                    lo, a + swap(b), swap(c) + d
                )
        sends[...] = spec_f[...].reshape(NQ, 2 * ZL, LANES).astype(BF)

    def y_synthesis(table, spec):
        spec_f[...] = spec[...].astype(F32).reshape(vrows, LANES)
        for pair in range(ZL // 2):
            two = []
            for i in range(2):
                value = spec_f[pl.ds(2 * pair + i, modes, stride=ZL), :]
                other = swap(value)
                two.append(
                    jnp.concatenate(
                        [
                            jnp.where(lo, value, 0.0), jnp.where(lo, 0.0, other),
                            jnp.where(lo, other, 0.0), jnp.where(lo, 0.0, value),
                        ],
                        0,
                    )
                )
            both = jnp.concatenate(two, 1).astype(BF)
            cells = dot_nn(table[...], jnp.concatenate([both, both], 0))
            for i in range(2):
                cells_f[pl.ds(2 * pair + i, 3 * NP, stride=ZL), :] = cells[
                    :, i * LANES:(i + 1) * LANES
                ]

    def z_analysis(table, landing, store):
        both = table[...]
        for h in range(2):
            block = landing[:, h].astype(F32)
            for j in range(3):
                cells = block[:, j * ZL:(j + 1) * ZL].reshape(NQ * ZL, LANES).astype(BF)
                spec = dot_nn(both, jnp.concatenate([cells, cells], 0))
                re, im = spec[:modes], spec[modes:]
                at = (h * 3 + j) * 2 * modes
                store[pl.ds(at, modes), :] = jnp.where(lo, re, swap(im))
                store[pl.ds(at + modes, modes), :] = jnp.where(lo, swap(re), im)

    def z_synthesis(table, source, sends):
        three = table[...]
        for h in range(2):
            out = []
            for j in range(3):
                at = (h * 3 + j) * 2 * modes
                even, odd = source[pl.ds(at, modes), :], source[pl.ds(at + modes, modes), :]
                spec = jnp.concatenate(
                    [jnp.where(lo, even, swap(odd)), jnp.where(lo, swap(even), odd)], 0
                )
                sh, sl = parts_of(spec)
                cells = dot_nn(three, jnp.concatenate([sh, sl, sh], 0))
                out.append(cells.reshape(NQ, ZL, LANES))
            sends[:, h] = jnp.concatenate(out, 1).astype(BF)

    unroll = min(8, modes)

    def z_split(source, sends):
        @pl.loop(0, modes // unroll)
        def _(step):
            for j in range(unroll):
                k = step * unroll + j
                sends[k] = source[pl.ds(k, 16, stride=modes), :].astype(BF)

    def z_mix(source, store, transposed):
        @pl.loop(0, modes // unroll)
        def _(step):
            for j in range(unroll):
                k = step * unroll + j
                high, low = parts_of(source[pl.ds(k, 16, stride=modes), :])
                both = jnp.concatenate([high, low], 0)
                got = dot_nt(both, mz[k]) if transposed else dot_nn(both, mz[k])
                store[pl.ds(k, 16, stride=modes), :] = got[:16] + got[16:]

    def fold(outer):
        top, bottom = outer[:64], swap(outer[64:])
        return top + jnp.where(lo, bottom, -bottom)

    second = (lax.broadcasted_iota(jnp.int32, (vrows, 1), 0) // ZL) % 2 == 1

    def y_mix(landing, dot):
        value = landing[...].reshape(vrows, LANES)
        return jnp.where(second, dot(value, my[1]), dot(value, my[0])).astype(BF).reshape(
            NQ, 2 * ZL, LANES
        )

    quarter = NQ // 2

    @pl.loop(0, quarter)
    def _(i):
        far = quarter // 2 + (1 - 2 * lax.rem(i, 2)) * ((i + 1) // 2)
        step = lax.rem(lax.rem(p, half) // 2 + far + quarter, quarter)
        for side in (0, 1):
            t = step + lax.rem(p // half + 1 + side, 2) * quarter
            for n in range(2):
                block = 2 * t + n

                @pl.when(block != p)
                def _():
                    at = r1.at[block]
                    pltpu.make_async_remote_copy(
                        src_ref=at,
                        dst_ref=at,
                        send_sem=send_sem.at[0],
                        recv_sem=state_sem.at[block],
                        device_id=(p, q),
                        device_id_type=MESH,
                    ).wait_recv()

            @pl.when(t != q)
            def _():
                pltpu.make_async_remote_copy(
                    src_ref=r1.at[pl.ds(2 * t, 2)],
                    dst_ref=z1.at[q],
                    send_sem=send_sem.at[1],
                    recv_sem=recv_sem.at[1],
                    device_id=(p, t),
                    device_id_type=MESH,
                ).start()

    pending.append((1, z1, NQ))
    own(z1, q, r1[pl.ds(2 * q, 2)].reshape(1, 2, 24, LANES))
    y_analysis(ytab.at[0], r1, y1s)
    send("pz", 3, lambda t: y1s.at[t], y1, NQ)
    send("py", 2, lambda t: cs.at[t], c1, NP)
    own(c1, p, cs[pl.ds(p, 1)])
    own(y1, q, y1s[pl.ds(q, 1)])
    arrived(1, z1, NQ)
    z_analysis(ztab.at[0], z1, uz)
    z_mix(uz, vz, False)
    z_synthesis(ztabt.at[1], vz, z2s)
    send("pz", 5, lambda t: z2s.at[t], z2, NQ)
    own(z2, q, z2s[pl.ds(q, 1)])
    arrived(3, y1, NQ)
    y2s[...] = y_mix(y1, dot_nn)
    send("pz", 4, lambda t: y2s.at[t], y2, NQ)
    own(y2, q, y2s[pl.ds(q, 1)])
    z_split(uz, us)
    send("pz", 17, lambda t: us.at[pl.ds(2 * t, 2)], ur, NQ)
    own(ur, q, us[pl.ds(2 * q, 2)].reshape(1, 2, 16, LANES))
    arrived(4, y2, NQ)
    y_synthesis(ytabt.at[1], y2)
    arrived(5, z2, NQ)
    mixb[...] = (cells_f[...].astype(BF).astype(F32) + lines(z2[...])).astype(BF)

    arrived(2, c1, NP)
    cotb[...] = lines(c1[...]).astype(BF)
    chunks = min(4, NQ)
    per = rows // chunks
    tile = 32 if per % 32 == 0 else 16
    root = math.sqrt(2.0 / math.pi)

    @pl.loop(0, chunks)
    def _(turn):
        chunk = lax.rem(turn + 1 + q // (NQ // chunks), chunks)
        start = pl.multiple_of(chunk * per, per)
        pre[...] = dot_nn(mixb[pl.ds(start, per), :], wi2[...])
        gact[...] = dot_nn(cotb[pl.ds(start, per), :], wo2[...])

        @pl.loop(0, per // tile)
        def _(step):
            here = pl.ds(pl.multiple_of(step * tile, tile), tile)
            at = pl.ds(pl.multiple_of(start + step * tile, tile), tile)
            value = pre[here, :]
            square = value * value
            bend = jnp.tanh(value * (root + (root * 0.044715) * square))
            rise = 0.5 + 0.5 * bend
            slope = rise + (0.5 * value) * (1.0 - bend * bend) * (
                root + (3.0 * root * 0.044715) * square
            )
            actb[at, :] = (value * rise).astype(BF)
            gpb[at, :] = (gact[here, :] * slope).astype(BF)

        back = dot_nt(gpb[pl.ds(start, per), :], wi2[...])
        g1[pl.ds(chunk * (NP // chunks), NP // chunks)] = back.reshape(
            NP // chunks, 24, LANES
        ).astype(BF)

        @pl.loop(0, NQ // chunks)
        def _(n):
            t = chunk * (NQ // chunks) + n

            @pl.when(t != q)
            def _():
                pltpu.make_async_remote_copy(
                    src_ref=g1.at[pl.ds(2 * t, 2)],
                    dst_ref=z3.at[q],
                    send_sem=send_sem.at[6],
                    recv_sem=recv_sem.at[6],
                    device_id=(p, t),
                    device_id_type=MESH,
                ).start()

    pending.append((6, z3, NQ))
    own(z3, q, g1[pl.ds(2 * q, 2)].reshape(1, 2, 24, LANES))
    y_analysis(ytab.at[1], g1, y3s)
    send("pz", 7, lambda t: y3s.at[t], y3, NQ)
    own(y3, q, y3s[pl.ds(q, 1)])

    def diagonal(both):
        return both[:64, :HID] + both[64:, HID:]

    dwi = diagonal(dot_tn(mixb[...], gpb[...]))
    dwo = diagonal(dot_tn(cotb[...], actb[...]))
    m1s[...] = jnp.concatenate(
        [dwi[:, :LANES], dwi[:, LANES:], dwo[:, :LANES], dwo[:, LANES:]], 0
    ).reshape(NP, share, LANES).astype(BF)
    send("py", 8, lambda t: m1s.at[t], m1r, NP)
    own(m1r, p, m1s[pl.ds(p, 1)])

    arrived(6, z3, NQ)
    z_analysis(ztab.at[1], z3, gz)
    z_split(gz, gs)
    send("pz", 10, lambda t: gs.at[pl.ds(2 * t, 2)], gr, NQ)
    own(gr, q, gs[pl.ds(2 * q, 2)].reshape(1, 2, 16, LANES))
    arrived(7, y3, NQ)
    y4s[...] = y_mix(y3, dot_nt)
    send("pz", 9, lambda t: y4s.at[t], y4, NQ)
    own(y4, q, y4s[pl.ds(q, 1)])

    for landing, store in ((y1, su), (y3, sg)):
        value = landing[...].astype(F32)
        for j in range(2):
            at = value[:, j * ZL:(j + 1) * ZL]
            store[j] = at.reshape(NQ * ZL, LANES).astype(BF)

    @pl.loop(0, 2)
    def _(j):
        dws[j] = fold(dot_tn(su[j], sg[j]))

    def scatter(branch, slot):
        out = [[], []]
        for j in range(2):
            even, odd = (dws[2 * branch + j, pl.ds(n, 32, stride=2), :] for n in range(2))
            out[0].append(jnp.where(lo, even, swap(odd)))
            out[1].append(jnp.where(lo, swap(even), odd))
        ws[branch] = jnp.concatenate(out[0] + out[1], 0).reshape(half, share, LANES).astype(BF)
        send(branch, slot, lambda t: ws.at[branch, t - branch * half], wr, NP)

        @pl.when(p // half == branch)
        def _():
            own(wr, p, ws[branch, pl.ds(p - branch * half, 1)])

    def gather(branch, slot, into, scale):
        @pl.when(p // half == branch)
        def _():
            arrived(slot, wr, NP)
            wg[...] = (jnp.sum(wr[...].astype(F32), axis=0) * scale).astype(BF)
            own(parts.at[branch], p - branch * half, wg[...].reshape(1, share, LANES))

            @pl.loop(0, half)
            def _(i):
                far = half // 2 + (1 - 2 * lax.rem(i, 2)) * ((i + 1) // 2)
                step = lax.rem(p + far + half, half)
                for side in (0, 1):
                    t = step + lax.rem(branch + 1 + side, 2) * half

                    @pl.when(t != p)
                    def _():
                        pltpu.make_async_remote_copy(
                            src_ref=wg,
                            dst_ref=parts.at[branch, p - branch * half],
                            send_sem=send_sem.at[into],
                            recv_sem=recv_sem.at[into],
                            device_id=(t, q),
                            device_id_type=MESH,
                        ).start()

    def settle(branch, slot, into):
        @pl.when(p // half == branch)
        def _():
            drain(slot, ws.at[branch], half).wait_send()
            drain(into, wr, NP).wait_send()

        @pl.when(p // half != branch)
        def _():
            drain(slot, ws.at[branch], half + 1).wait_send()

    scatter(0, 13)
    z_mix(gz, vz, True)
    z_synthesis(ztabt.at[0], vz, z4s)
    send("pz", 11, lambda t: z4s.at[t], z4, NQ)
    own(z4, q, z4s[pl.ds(q, 1)])
    arrived(17, ur, NQ)
    arrived(10, gr, NQ)

    @pl.loop(0, 2)
    def _(j):
        dws[2 + j] = fold(
            dot_tn(ur[:, j].reshape(NQ * 16, LANES), gr[:, j].reshape(NQ * 16, LANES))
        )

    scatter(1, 15)
    arrived(8, m1r, NP)
    own(m2r, q, jnp.sum(m1r[...].astype(F32), axis=0, keepdims=True))
    send("pz", 14, lambda t: m2r.at[q], m2r, NQ)

    arrived(9, y4, NQ)
    y_synthesis(ytabt.at[0], y4)
    arrived(11, z4, NQ)
    total = lines(c1[...]) + cells_f[...].astype(BF).astype(F32) + lines(z4[...])
    o1[...] = total.reshape(NP, 24, LANES).astype(BF)
    scale_y = 1.0 / math.sqrt(NP * ZL * NQ)
    scale_z = 1.0 / math.sqrt(NP * YL * NP)
    scale_mlp = 1.0 / math.sqrt(NP * (YL * NP) * (ZL * NQ))
    gather(0, 13, 16, scale_y)
    send("py", 12, lambda t: o1.at[t], f1, NP, (0, half // 2))
    own(f1, p, o1[pl.ds(p, 1)])
    gather(1, 15, 18, scale_z)
    send("py", 12, lambda t: o1.at[t], f1, NP, (half // 2, half))
    arrived(14, m2r, NQ)
    own(m3r, p, (jnp.sum(m2r[...], axis=0, keepdims=True) * scale_mlp).astype(BF))
    send("py", 19, lambda t: m3r.at[p], m3r, NP)

    targets = (grad_sy, grad_sz)

    def ring(branch, slot, device):
        at = targets[branch].at[:, slot]
        return pltpu.make_async_remote_copy(
            src_ref=at,
            dst_ref=at,
            send_sem=send_sem.at[20 + branch],
            recv_sem=ring_sem.at[branch, slot],
            device_id=(p, device),
            device_id_type=MESH,
        )

    def ring_start(branch, into):
        @pl.when(p // half == branch)
        def _():
            drain(into, parts.at[branch], half).wait_recv()

        @pl.when(p // half != branch)
        def _():
            drain(into, parts.at[branch], half + 1).wait_recv()

        whole = parts[branch].astype(F32).reshape(2, 1, CH, LANES).astype(BF)
        targets[branch][:, pl.ds(q, 1)] = whole

        @pl.loop(1, NQ // 2)
        def _(j):
            ring(branch, q, lax.rem(q + 2 * j, NQ)).start()

        ring(branch, q, sibling).start()

    def ring_pass(branch):
        @pl.loop(1, NQ // 2)
        def _(j):
            slot = lax.rem(q + 2 * j, NQ)
            ring(branch, slot, sibling).wait_recv()
            ring(branch, slot, sibling).start()

    def ring_end(branch):
        @pl.loop(0, NQ // 2)
        def _(j):
            ring(branch, lax.rem(sibling + 2 * j, NQ), sibling).wait_recv()

    ring_start(0, 16)
    ring_start(1, 18)
    ring_pass(0)
    arrived(12, f1, NP)
    from_blocks(f1, grad_state)
    ring_pass(1)
    arrived(19, m3r, NP)
    small = m3r[...].reshape(256, LANES)
    grad_in[...] = jnp.concatenate([small[:64], small[64:128]], 1)
    grad_out[...] = jnp.concatenate([small[128:192], small[192:]], 1)
    ring_end(0)
    ring_end(1)

    for item in pending:
        drain(*item).wait_send()
    settle(0, 13, 16)
    settle(1, 15, 18)
    for branch in range(2):
        span = targets[branch].at[:, pl.ds(0, NQ - 1)]
        pltpu.make_async_remote_copy(
            src_ref=span,
            dst_ref=span,
            send_sem=send_sem.at[20 + branch],
            recv_sem=ring_sem.at[branch, 0],
            device_id=(p, q),
            device_id_type=MESH,
        ).wait_send()


def on_device(NP, NQ, state, cotangent, spectral_y, spectral_z, w_in, w_out):
    modes = 2 * NQ
    rows = NP * 24
    vrows = modes * ZL
    share = 256 // NP

    forward_y, inverse_y = base_tables(YL * NP, modes)
    forward_z, inverse_z = base_tables(ZL * NQ, modes)
    yf = np_parts(y_tables(forward_y, NP, modes))
    ya = np_parts(y_tables(inverse_y, NP, modes))
    zf = np_parts(np.concatenate(forward_z, 0))
    za = np_parts(np.concatenate(inverse_z, 0))
    flip = lambda pair: [v.T for v in pair]
    tables = [
        np.stack([np.concatenate(v, 1) for v in (yf, ya)]),
        np.stack([np.concatenate(flip(v), 1) for v in (yf, ya)]),
        np.stack([np.concatenate(v, 1) for v in (zf, za)]),
        np.stack([np.concatenate([v[0].T, v[0].T, v[1].T], 1) for v in (zf, za)]),
    ]

    vmem = pl.BlockSpec(memory_space=pltpu.VMEM)
    V = pltpu.VMEM
    field = lambda: V((NP, 24, LANES), BF)
    zbuf = lambda: V((NQ, 2, 24, LANES), BF)
    ybuf = lambda: V((NQ, 2 * ZL, LANES), BF)
    pack = lambda kind: V((NP, share, LANES), kind)
    scratch = [
        field(), field(), field(), field(), zbuf(), ybuf(), ybuf(), ybuf(), ybuf(), zbuf(), zbuf(),
        field(), zbuf(), ybuf(), ybuf(), ybuf(), ybuf(), zbuf(), zbuf(), field(), field(),
        V((modes, 16, LANES), BF), V((NQ, 2, 16, LANES), BF),
        V((modes, 16, LANES), BF), V((NQ, 2, 16, LANES), BF),
        V((2, NP // 2, share, LANES), BF), pack(BF), V((share, LANES), BF),
        V((2, NP // 2, share, LANES), BF),
        pack(BF), pack(BF), V((NQ, share, LANES), F32), pack(BF),
        V((LANES, 2 * HID), BF), V((LANES, 2 * HID), BF),
        V((2, LANES, LANES), BF), V((modes, LANES, LANES), BF),
        V((rows // min(4, NQ), 2 * HID), F32), V((rows // min(4, NQ), 2 * HID), F32),
        V((rows, 2 * HID), BF), V((rows, 2 * HID), BF), V((rows, LANES), BF), V((rows, LANES), BF),
        V((16 * modes, LANES), F32), V((16 * modes, LANES), F32), V((16 * modes, LANES), F32),
        V((2, NQ * ZL, LANES), BF), V((2, NQ * ZL, LANES), BF), V((4, CH, LANES), F32),
        V((rows, LANES), F32), V((vrows, LANES), F32),
        V((ZL * NP, LANES), F32),
        V((max(modes * LANES, rows), LANES), F32),
        V((2, 2, modes, CH * CH), BF),
        V((YL, CH, ZL * NP), BF), V((YL, CH, ZL * NP), BF), V((CH, HID), BF), V((CH, HID), BF),
        *[V(t.shape, BF) for t in tables],
        pltpu.SemaphoreType.DMA((22,)),
        pltpu.SemaphoreType.DMA((22,)),
        pltpu.SemaphoreType.DMA((2, NQ)),
        pltpu.SemaphoreType.DMA((10,)),
        pltpu.SemaphoreType.DMA((NP,)),
    ]
    state, cotangent = (jnp.transpose(v, (1, 0, 2)) for v in (state, cotangent))
    shape = lambda like: V(like.shape, BF)
    spec = V((2, NQ, CH, LANES), BF)
    grad, grad_sy, grad_sz, grad_in, grad_out = pl.pallas_call(
        functools.partial(kernel, NP, NQ),
        out_shape=(shape(state), spec, spec, shape(w_in), shape(w_in)),
        in_specs=[pl.BlockSpec(memory_space=pl.ANY)] * (6 + len(tables)),
        out_specs=(vmem,) * 5,
        scratch_shapes=scratch,
        compiler_params=pltpu.CompilerParams(
            collective_id=0, has_side_effects=True, vmem_limit_bytes=56 * 1024 * 1024
        ),
    )(state, cotangent, spectral_y, spectral_z, w_in, w_out.T, *[jnp.asarray(t) for t in tables])
    grad_sy, grad_sz = (v.reshape(2, modes, CH * CH) for v in (grad_sy, grad_sz))
    return (jnp.transpose(grad, (1, 0, 2)), grad_sy, grad_sz, grad_in, grad_out.T)


def solution(mesh):
    sizes = (mesh.shape["py"], mesh.shape["pz"])
    in_specs = (P(None, "py", "pz"), P(None, "py", "pz"), P(), P(), P(), P())
    out_specs = (P(None, "py", "pz"), P(), P(), P(), P())
    return jax.shard_map(
        functools.partial(on_device, *sizes),
        mesh=mesh,
        in_specs=in_specs,
        out_specs=out_specs,
        check_vma=False,
    )
```

```python
import functools
import math

import jax
import jax.numpy as jnp
import numpy as np
from jax import lax
from jax.experimental import pallas as pl
from jax.experimental.pallas import tpu as pltpu
from jax.sharding import PartitionSpec as P

MESH = pl.DeviceIdType.MESH
BF, F32 = jnp.bfloat16, jnp.float32
CH, HID = 64, 256
YL, ZL = 6, 8
LANES = 128


def dot_nn(a, b):
    return lax.dot_general(a, b, (((1,), (0,)), ((), ())), preferred_element_type=F32)


def dot_nt(a, b):
    return lax.dot_general(a, b, (((1,), (1,)), ((), ())), preferred_element_type=F32)


def dot_tn(a, b):
    return lax.dot_general(a, b, (((0,), (0,)), ((), ())), preferred_element_type=F32)


def parts_of(value):
    high = value.astype(BF)
    return high, (value - high.astype(F32)).astype(BF)


def np_parts(table):
    high = table.astype(np.float32).astype(BF)
    low = (table - high.astype(np.float64)).astype(np.float32).astype(BF)
    return high, low


def base_tables(length, modes):
    phase = 2.0 * np.pi * (np.outer(np.arange(modes), np.arange(length)) % length) / length
    weight = np.where(np.arange(modes) == 0, 1.0, 2.0)[:, None] / length
    forward = (np.cos(phase), -np.sin(phase))
    inverse = (weight * np.cos(phase), -weight * np.sin(phase))
    return forward, inverse


def y_tables(pair, spans, modes):
    cuts = [table.reshape(modes, spans * 3, 2) for table in pair]
    return np.concatenate([cut[..., odd] for cut in cuts for odd in range(2)], 0)


def swap(value):
    return pltpu.roll(value, 64, 1)


def kernel(
    NP,
    NQ,
    state_in, cot_in, spectral_y, spectral_z, w_in_hbm, w_out_hbm, ytab_hbm, ytabt_hbm, ztab_hbm, ztabt_hbm,
    grad_state, grad_sy, grad_sz, grad_in, grad_out,
    xs, cs, r1, c1, z1, y1s, y1, y2s, y2, z2s, z2, g1, z3, y3s, y3, y4s, y4, z4s, z4, o1, f1,
    us, ur, gs, gr, ws, wr, wg, parts, m1s, m1r, m2r, m3r,
    wi2, wo2, my, mz, pre, gact, actb, gpb, mixb, cotb, uz, gz, vz, su, sg, dws,
    cells_f, spec_f, turn_f, big_f,
    weights_f, state, cotangent, w_in, w_out, ytab, ytabt, ztab, ztabt,
    send_sem, recv_sem, ring_sem, fetch_sem, state_sem,
):
    modes = 2 * NQ
    rows = NP * 24
    vrows = modes * ZL
    share = 256 // NP
    half = NP // 2
    p, q = lax.axis_index("py"), lax.axis_index("pz")
    sibling = q + 1 - 2 * lax.rem(q, 2)

    barrier = pltpu.get_barrier_semaphore()

    @pl.loop(1, NP)
    def _(i):
        pl.semaphore_signal(barrier, inc=1, device_id=(lax.rem(p + i, NP), q), device_id_type=MESH)

    @pl.loop(1, NQ)
    def _(i):
        pl.semaphore_signal(barrier, inc=1, device_id=(p, lax.rem(q + i, NQ)), device_id_type=MESH)

    lo = lax.broadcasted_iota(jnp.int32, (1, LANES), 1) < 64
    pending = []

    def send(kind, slot, source, landing, n, span=(0, half), each=None):
        def start(t, mine, device):
            pltpu.make_async_remote_copy(
                src_ref=source(t),
                dst_ref=landing.at[mine],
                send_sem=send_sem.at[slot],
                recv_sem=recv_sem.at[slot] if each is None else each.at[mine],
                device_id=device,
                device_id_type=MESH,
            ).start()

        if kind == "pz":

            @pl.loop(1, n)
            def _(i):
                t = lax.rem(q + i, n)
                start(t, q, (p, t))

        else:

            @pl.loop(*span)
            def _(i):
                far = half // 2 + (1 - 2 * lax.rem(i, 2)) * ((i + 1) // 2)
                step = lax.rem(p + far + half, half)
                sides = (0, 1) if kind == "py" else (kind,)
                for side in sides:
                    t = step + (lax.rem(p // half + 1 + side, 2) if kind == "py" else side) * half

                    @pl.when(t != p)
                    def _():
                        start(t, p, (t, q))

            if span[1] < half or kind != "py":
                return

        pending.append((slot, landing, n))

    def drain(slot, landing, n):
        span = landing.at[pl.ds(0, n - 1)]
        return pltpu.make_async_remote_copy(
            src_ref=span,
            dst_ref=span,
            send_sem=send_sem.at[slot],
            recv_sem=recv_sem.at[slot],
            device_id=(p, q),
            device_id_type=MESH,
        )

    def arrived(slot, landing, n):
        drain(slot, landing, n).wait_recv()

    def own(landing, at, value):
        landing[pl.ds(at, 1)] = value

    def to_blocks(source, blocks):
        for j in range(3):
            turn_f[...] = jnp.concatenate([source[2 * j], source[2 * j + 1]], 0).astype(F32).T
            for x in range(NP):
                big_f[pl.ds(x * 24 + j * ZL, ZL), :] = turn_f[pl.ds(x, ZL, stride=NP), :]
        blocks[...] = big_f[:rows, :].reshape(NP, 24, LANES).astype(BF)

    def from_blocks(blocks, target):
        big_f[:rows, :] = blocks[...].astype(F32).reshape(rows, LANES)
        for j in range(3):
            cells = [big_f[pl.ds(j * ZL + z, NP, stride=24), :] for z in range(ZL)]
            turned = jnp.concatenate(cells, 0).T.astype(BF)
            target[2 * j] = turned[:64]
            target[2 * j + 1] = turned[64:]

    def mixing(weights):
        @pl.loop(0, 8)
        def _(step):
            for n in range(4):
                g = step * 4 + n
                at = pl.ds(pl.multiple_of(g * LANES, LANES), LANES)
                re, im = weights[0, :, at].astype(F32), weights[1, :, at].astype(F32)
                re_s, im_s = swap(re), swap(im)
                big_f[pl.ds(2 * g, modes, stride=LANES), :] = jnp.where(lo, re, im_s)
                big_f[pl.ds(2 * g + 1, modes, stride=LANES), :] = jnp.where(lo, re_s, im)
                big_f[pl.ds(64 + 2 * g, modes, stride=LANES), :] = jnp.where(lo, -im, re_s)
                big_f[pl.ds(65 + 2 * g, modes, stride=LANES), :] = jnp.where(lo, -im_s, re)

    fetches = [
        pltpu.make_async_copy(source, target, fetch_sem.at[n])
        for n, (source, target) in enumerate(
            [
                (state_in, state), (cot_in, cotangent),
                (spectral_z, weights_f.at[0]), (spectral_y, weights_f.at[1]),
                (w_in_hbm, w_in), (w_out_hbm, w_out),
                (ytab_hbm, ytab), (ytabt_hbm, ytabt), (ztab_hbm, ztab), (ztabt_hbm, ztabt),
            ]
        )
    ]
    for fetch in fetches:
        fetch.start()
    fetches[0].wait()
    to_blocks(state, xs)
    pl.semaphore_wait(barrier, NP - 1 + NQ - 1)

    send("py", 0, lambda t: xs.at[t], r1, NP, each=state_sem)
    own(r1, p, xs[pl.ds(p, 1)])
    fetches[1].wait()
    to_blocks(cotangent, cs)
    for fetch in fetches[2:]:
        fetch.wait()
    mixing(weights_f.at[0])

    @pl.loop(0, modes)
    def _(k):
        mz[k] = big_f[pl.ds(pl.multiple_of(k * LANES, LANES), LANES), :].astype(BF)

    mixing(weights_f.at[1])
    for j in range(2):
        my[j] = big_f[pl.ds(pl.multiple_of((2 * q + j) * LANES, LANES), LANES), :].astype(BF)
    wi2[...] = jnp.zeros_like(wi2)
    wo2[...] = jnp.zeros_like(wo2)
    for j in range(2):
        wi2[j * 64:(j + 1) * 64, j * HID:(j + 1) * HID] = w_in[...]
        wo2[j * 64:(j + 1) * 64, j * HID:(j + 1) * HID] = w_out[...]
    uz[...] = jnp.zeros_like(uz)
    gz[...] = jnp.zeros_like(gz)
    def lines(block):
        return block.astype(F32).reshape(rows, LANES)

    def y_analysis(table, field, sends):
        cells_f[...] = lines(field[...])
        for pair in range(ZL // 2):
            two = [cells_f[pl.ds(2 * pair + i, 3 * NP, stride=ZL), :] for i in range(2)]
            both = jnp.concatenate(two, 1).astype(BF)
            spec = dot_nn(table[...], jnp.concatenate([both, both], 0))
            for i in range(2):
                a, b, c, d = (
                    spec[n * modes:(n + 1) * modes, i * LANES:(i + 1) * LANES] for n in range(4)
                )
                spec_f[pl.ds(2 * pair + i, modes, stride=ZL), :] = jnp.where(
                    lo, a + swap(b), swap(c) + d
                )
        sends[...] = spec_f[...].reshape(NQ, 2 * ZL, LANES).astype(BF)

    def y_synthesis(table, spec):
        spec_f[...] = spec[...].astype(F32).reshape(vrows, LANES)
        for pair in range(ZL // 2):
            two = []
            for i in range(2):
                value = spec_f[pl.ds(2 * pair + i, modes, stride=ZL), :]
                other = swap(value)
                two.append(
                    jnp.concatenate(
                        [
                            jnp.where(lo, value, 0.0), jnp.where(lo, 0.0, other),
                            jnp.where(lo, other, 0.0), jnp.where(lo, 0.0, value),
                        ],
                        0,
                    )
                )
            both = jnp.concatenate(two, 1).astype(BF)
            cells = dot_nn(table[...], jnp.concatenate([both, both], 0))
            for i in range(2):
                cells_f[pl.ds(2 * pair + i, 3 * NP, stride=ZL), :] = cells[
                    :, i * LANES:(i + 1) * LANES
                ]

    def z_analysis(table, landing, store):
        both = table[...]
        for h in range(2):
            block = landing[:, h].astype(F32)
            for j in range(3):
                cells = block[:, j * ZL:(j + 1) * ZL].reshape(NQ * ZL, LANES).astype(BF)
                spec = dot_nn(both, jnp.concatenate([cells, cells], 0))
                re, im = spec[:modes], spec[modes:]
                at = (h * 3 + j) * 2 * modes
                store[pl.ds(at, modes), :] = jnp.where(lo, re, swap(im))
                store[pl.ds(at + modes, modes), :] = jnp.where(lo, swap(re), im)

    def z_synthesis(table, source, sends):
        three = table[...]
        for h in range(2):
            out = []
            for j in range(3):
                at = (h * 3 + j) * 2 * modes
                even, odd = source[pl.ds(at, modes), :], source[pl.ds(at + modes, modes), :]
                spec = jnp.concatenate(
                    [jnp.where(lo, even, swap(odd)), jnp.where(lo, swap(even), odd)], 0
                )
                sh, sl = parts_of(spec)
                cells = dot_nn(three, jnp.concatenate([sh, sl, sh], 0))
                out.append(cells.reshape(NQ, ZL, LANES))
            sends[:, h] = jnp.concatenate(out, 1).astype(BF)

    unroll = min(8, modes)

    def z_split(source, sends):
        @pl.loop(0, modes // unroll)
        def _(step):
            for j in range(unroll):
                k = step * unroll + j
                sends[k] = source[pl.ds(k, 16, stride=modes), :].astype(BF)

    def z_mix(source, store, transposed):
        @pl.loop(0, modes // unroll)
        def _(step):
            for j in range(unroll):
                k = step * unroll + j
                high, low = parts_of(source[pl.ds(k, 16, stride=modes), :])
                both = jnp.concatenate([high, low], 0)
                got = dot_nt(both, mz[k]) if transposed else dot_nn(both, mz[k])
                store[pl.ds(k, 16, stride=modes), :] = got[:16] + got[16:]

    def fold(outer):
        top, bottom = outer[:64], swap(outer[64:])
        return top + jnp.where(lo, bottom, -bottom)

    second = (lax.broadcasted_iota(jnp.int32, (vrows, 1), 0) // ZL) % 2 == 1

    def y_mix(landing, dot):
        value = landing[...].reshape(vrows, LANES)
        return jnp.where(second, dot(value, my[1]), dot(value, my[0])).astype(BF).reshape(
            NQ, 2 * ZL, LANES
        )

    quarter = NQ // 2

    @pl.loop(0, quarter)
    def _(i):
        far = quarter // 2 + (1 - 2 * lax.rem(i, 2)) * ((i + 1) // 2)
        step = lax.rem(lax.rem(p, half) // 2 + far + quarter, quarter)
        for side in (0, 1):
            t = step + lax.rem(p // half + 1 + side, 2) * quarter
            for n in range(2):
                block = 2 * t + n

                @pl.when(block != p)
                def _():
                    at = r1.at[block]
                    pltpu.make_async_remote_copy(
                        src_ref=at,
                        dst_ref=at,
                        send_sem=send_sem.at[0],
                        recv_sem=state_sem.at[block],
                        device_id=(p, q),
                        device_id_type=MESH,
                    ).wait_recv()

            @pl.when(t != q)
            def _():
                pltpu.make_async_remote_copy(
                    src_ref=r1.at[pl.ds(2 * t, 2)],
                    dst_ref=z1.at[q],
                    send_sem=send_sem.at[1],
                    recv_sem=recv_sem.at[1],
                    device_id=(p, t),
                    device_id_type=MESH,
                ).start()

    pending.append((1, z1, NQ))
    own(z1, q, r1[pl.ds(2 * q, 2)].reshape(1, 2, 24, LANES))
    y_analysis(ytab.at[0], r1, y1s)
    send("pz", 3, lambda t: y1s.at[t], y1, NQ)
    send("py", 2, lambda t: cs.at[t], c1, NP)
    own(c1, p, cs[pl.ds(p, 1)])
    own(y1, q, y1s[pl.ds(q, 1)])
    arrived(1, z1, NQ)
    z_analysis(ztab.at[0], z1, uz)
    z_mix(uz, vz, False)
    z_synthesis(ztabt.at[1], vz, z2s)
    send("pz", 5, lambda t: z2s.at[t], z2, NQ)
    own(z2, q, z2s[pl.ds(q, 1)])
    arrived(3, y1, NQ)
    y2s[...] = y_mix(y1, dot_nn)
    send("pz", 4, lambda t: y2s.at[t], y2, NQ)
    own(y2, q, y2s[pl.ds(q, 1)])
    z_split(uz, us)
    send("pz", 17, lambda t: us.at[pl.ds(2 * t, 2)], ur, NQ)
    own(ur, q, us[pl.ds(2 * q, 2)].reshape(1, 2, 16, LANES))
    arrived(4, y2, NQ)
    y_synthesis(ytabt.at[1], y2)
    arrived(5, z2, NQ)
    mixb[...] = (cells_f[...].astype(BF).astype(F32) + lines(z2[...])).astype(BF)

    arrived(2, c1, NP)
    cotb[...] = lines(c1[...]).astype(BF)
    chunks = min(4, NQ)
    per = rows // chunks
    tile = 32 if per % 32 == 0 else 16
    root = math.sqrt(2.0 / math.pi)

    @pl.loop(0, chunks)
    def _(turn):
        chunk = lax.rem(turn + 1 + q // (NQ // chunks), chunks)
        start = pl.multiple_of(chunk * per, per)
        pre[...] = dot_nn(mixb[pl.ds(start, per), :], wi2[...])
        gact[...] = dot_nn(cotb[pl.ds(start, per), :], wo2[...])

        @pl.loop(0, per // tile)
        def _(step):
            here = pl.ds(pl.multiple_of(step * tile, tile), tile)
            at = pl.ds(pl.multiple_of(start + step * tile, tile), tile)
            value = pre[here, :]
            square = value * value
            bend = jnp.tanh(value * (root + (root * 0.044715) * square))
            rise = 0.5 + 0.5 * bend
            slope = rise + (0.5 * value) * (1.0 - bend * bend) * (
                root + (3.0 * root * 0.044715) * square
            )
            actb[at, :] = (value * rise).astype(BF)
            gpb[at, :] = (gact[here, :] * slope).astype(BF)

        back = dot_nt(gpb[pl.ds(start, per), :], wi2[...])
        g1[pl.ds(chunk * (NP // chunks), NP // chunks)] = back.reshape(
            NP // chunks, 24, LANES
        ).astype(BF)

        @pl.loop(0, NQ // chunks)
        def _(n):
            t = chunk * (NQ // chunks) + n

            @pl.when(t != q)
            def _():
                pltpu.make_async_remote_copy(
                    src_ref=g1.at[pl.ds(2 * t, 2)],
                    dst_ref=z3.at[q],
                    send_sem=send_sem.at[6],
                    recv_sem=recv_sem.at[6],
                    device_id=(p, t),
                    device_id_type=MESH,
                ).start()

    pending.append((6, z3, NQ))
    own(z3, q, g1[pl.ds(2 * q, 2)].reshape(1, 2, 24, LANES))
    y_analysis(ytab.at[1], g1, y3s)
    send("pz", 7, lambda t: y3s.at[t], y3, NQ)
    own(y3, q, y3s[pl.ds(q, 1)])

    def diagonal(both):
        return both[:64, :HID] + both[64:, HID:]

    dwi = diagonal(dot_tn(mixb[...], gpb[...]))
    dwo = diagonal(dot_tn(cotb[...], actb[...]))
    m1s[...] = jnp.concatenate(
        [dwi[:, :LANES], dwi[:, LANES:], dwo[:, :LANES], dwo[:, LANES:]], 0
    ).reshape(NP, share, LANES).astype(BF)
    send("py", 8, lambda t: m1s.at[t], m1r, NP)
    own(m1r, p, m1s[pl.ds(p, 1)])

    arrived(6, z3, NQ)
    z_analysis(ztab.at[1], z3, gz)
    z_split(gz, gs)
    send("pz", 10, lambda t: gs.at[pl.ds(2 * t, 2)], gr, NQ)
    own(gr, q, gs[pl.ds(2 * q, 2)].reshape(1, 2, 16, LANES))
    arrived(7, y3, NQ)
    y4s[...] = y_mix(y3, dot_nt)
    send("pz", 9, lambda t: y4s.at[t], y4, NQ)
    own(y4, q, y4s[pl.ds(q, 1)])

    for landing, store in ((y1, su), (y3, sg)):
        value = landing[...].astype(F32)
        for j in range(2):
            at = value[:, j * ZL:(j + 1) * ZL]
            store[j] = at.reshape(NQ * ZL, LANES).astype(BF)

    @pl.loop(0, 2)
    def _(j):
        dws[j] = fold(dot_tn(su[j], sg[j]))

    def scatter(branch, slot):
        out = [[], []]
        for j in range(2):
            even, odd = (dws[2 * branch + j, pl.ds(n, 32, stride=2), :] for n in range(2))
            out[0].append(jnp.where(lo, even, swap(odd)))
            out[1].append(jnp.where(lo, swap(even), odd))
        ws[branch] = jnp.concatenate(out[0] + out[1], 0).reshape(half, share, LANES).astype(BF)
        send(branch, slot, lambda t: ws.at[branch, t - branch * half], wr, NP)

        @pl.when(p // half == branch)
        def _():
            own(wr, p, ws[branch, pl.ds(p - branch * half, 1)])

    def gather(branch, slot, into, scale):
        @pl.when(p // half == branch)
        def _():
            arrived(slot, wr, NP)
            wg[...] = (jnp.sum(wr[...].astype(F32), axis=0) * scale).astype(BF)
            own(parts.at[branch], p - branch * half, wg[...].reshape(1, share, LANES))

            @pl.loop(0, half)
            def _(i):
                far = half // 2 + (1 - 2 * lax.rem(i, 2)) * ((i + 1) // 2)
                step = lax.rem(p + far + half, half)
                for side in (0, 1):
                    t = step + lax.rem(branch + 1 + side, 2) * half

                    @pl.when(t != p)
                    def _():
                        pltpu.make_async_remote_copy(
                            src_ref=wg,
                            dst_ref=parts.at[branch, p - branch * half],
                            send_sem=send_sem.at[into],
                            recv_sem=recv_sem.at[into],
                            device_id=(t, q),
                            device_id_type=MESH,
                        ).start()

    def settle(branch, slot, into):
        @pl.when(p // half == branch)
        def _():
            drain(slot, ws.at[branch], half).wait_send()
            drain(into, wr, NP).wait_send()

        @pl.when(p // half != branch)
        def _():
            drain(slot, ws.at[branch], half + 1).wait_send()

    scatter(0, 13)
    z_mix(gz, vz, True)
    z_synthesis(ztabt.at[0], vz, z4s)
    send("pz", 11, lambda t: z4s.at[t], z4, NQ)
    own(z4, q, z4s[pl.ds(q, 1)])
    arrived(17, ur, NQ)
    arrived(10, gr, NQ)

    @pl.loop(0, 2)
    def _(j):
        dws[2 + j] = fold(
            dot_tn(ur[:, j].reshape(NQ * 16, LANES), gr[:, j].reshape(NQ * 16, LANES))
        )

    scatter(1, 15)
    arrived(8, m1r, NP)
    own(m2r, q, jnp.sum(m1r[...].astype(F32), axis=0, keepdims=True))
    send("pz", 14, lambda t: m2r.at[q], m2r, NQ)

    arrived(9, y4, NQ)
    y_synthesis(ytabt.at[0], y4)
    arrived(11, z4, NQ)
    total = lines(c1[...]) + cells_f[...].astype(BF).astype(F32) + lines(z4[...])
    o1[...] = total.reshape(NP, 24, LANES).astype(BF)
    scale_y = 1.0 / math.sqrt(NP * ZL * NQ)
    scale_z = 1.0 / math.sqrt(NP * YL * NP)
    scale_mlp = 1.0 / math.sqrt(NP * (YL * NP) * (ZL * NQ))
    gather(0, 13, 16, scale_y)
    send("py", 12, lambda t: o1.at[t], f1, NP, (0, half // 4))
    own(f1, p, o1[pl.ds(p, 1)])
    gather(1, 15, 18, scale_z)
    send("py", 12, lambda t: o1.at[t], f1, NP, (half // 4, half))
    arrived(14, m2r, NQ)
    own(m3r, p, (jnp.sum(m2r[...], axis=0, keepdims=True) * scale_mlp).astype(BF))
    send("py", 19, lambda t: m3r.at[p], m3r, NP)

    targets = (grad_sy, grad_sz)

    def ring(branch, slot, device):
        at = targets[branch].at[:, slot]
        return pltpu.make_async_remote_copy(
            src_ref=at,
            dst_ref=at,
            send_sem=send_sem.at[20 + branch],
            recv_sem=ring_sem.at[branch, slot],
            device_id=(p, device),
            device_id_type=MESH,
        )

    def ring_start(branch, into):
        @pl.when(p // half == branch)
        def _():
            drain(into, parts.at[branch], half).wait_recv()

        @pl.when(p // half != branch)
        def _():
            drain(into, parts.at[branch], half + 1).wait_recv()

        whole = parts[branch].astype(F32).reshape(2, 1, CH, LANES).astype(BF)
        targets[branch][:, pl.ds(q, 1)] = whole

        @pl.loop(1, NQ // 2)
        def _(j):
            ring(branch, q, lax.rem(q + 2 * j, NQ)).start()

        ring(branch, q, sibling).start()

    def ring_pass(branch):
        @pl.loop(1, NQ // 2)
        def _(j):
            slot = lax.rem(q + 2 * j, NQ)
            ring(branch, slot, sibling).wait_recv()
            ring(branch, slot, sibling).start()

    def ring_end(branch):
        @pl.loop(0, NQ // 2)
        def _(j):
            ring(branch, lax.rem(sibling + 2 * j, NQ), sibling).wait_recv()

    ring_start(0, 16)
    ring_start(1, 18)
    ring_pass(0)
    ring_pass(1)
    arrived(12, f1, NP)
    from_blocks(f1, grad_state)
    arrived(19, m3r, NP)
    small = m3r[...].reshape(256, LANES)
    grad_in[...] = jnp.concatenate([small[:64], small[64:128]], 1)
    grad_out[...] = jnp.concatenate([small[128:192], small[192:]], 1)
    ring_end(0)
    ring_end(1)

    for item in pending:
        drain(*item).wait_send()
    settle(0, 13, 16)
    settle(1, 15, 18)
    for branch in range(2):
        span = targets[branch].at[:, pl.ds(0, NQ - 1)]
        pltpu.make_async_remote_copy(
            src_ref=span,
            dst_ref=span,
            send_sem=send_sem.at[20 + branch],
            recv_sem=ring_sem.at[branch, 0],
            device_id=(p, q),
            device_id_type=MESH,
        ).wait_send()


def on_device(NP, NQ, state, cotangent, spectral_y, spectral_z, w_in, w_out):
    modes = 2 * NQ
    rows = NP * 24
    vrows = modes * ZL
    share = 256 // NP

    forward_y, inverse_y = base_tables(YL * NP, modes)
    forward_z, inverse_z = base_tables(ZL * NQ, modes)
    yf = np_parts(y_tables(forward_y, NP, modes))
    ya = np_parts(y_tables(inverse_y, NP, modes))
    zf = np_parts(np.concatenate(forward_z, 0))
    za = np_parts(np.concatenate(inverse_z, 0))
    flip = lambda pair: [v.T for v in pair]
    tables = [
        np.stack([np.concatenate(v, 1) for v in (yf, ya)]),
        np.stack([np.concatenate(flip(v), 1) for v in (yf, ya)]),
        np.stack([np.concatenate(v, 1) for v in (zf, za)]),
        np.stack([np.concatenate([v[0].T, v[0].T, v[1].T], 1) for v in (zf, za)]),
    ]

    vmem = pl.BlockSpec(memory_space=pltpu.VMEM)
    V = pltpu.VMEM
    field = lambda: V((NP, 24, LANES), BF)
    zbuf = lambda: V((NQ, 2, 24, LANES), BF)
    ybuf = lambda: V((NQ, 2 * ZL, LANES), BF)
    pack = lambda kind: V((NP, share, LANES), kind)
    scratch = [
        field(), field(), field(), field(), zbuf(), ybuf(), ybuf(), ybuf(), ybuf(), zbuf(), zbuf(),
        field(), zbuf(), ybuf(), ybuf(), ybuf(), ybuf(), zbuf(), zbuf(), field(), field(),
        V((modes, 16, LANES), BF), V((NQ, 2, 16, LANES), BF),
        V((modes, 16, LANES), BF), V((NQ, 2, 16, LANES), BF),
        V((2, NP // 2, share, LANES), BF), pack(BF), V((share, LANES), BF),
        V((2, NP // 2, share, LANES), BF),
        pack(BF), pack(BF), V((NQ, share, LANES), F32), pack(BF),
        V((LANES, 2 * HID), BF), V((LANES, 2 * HID), BF),
        V((2, LANES, LANES), BF), V((modes, LANES, LANES), BF),
        V((rows // min(4, NQ), 2 * HID), F32), V((rows // min(4, NQ), 2 * HID), F32),
        V((rows, 2 * HID), BF), V((rows, 2 * HID), BF), V((rows, LANES), BF), V((rows, LANES), BF),
        V((16 * modes, LANES), F32), V((16 * modes, LANES), F32), V((16 * modes, LANES), F32),
        V((2, NQ * ZL, LANES), BF), V((2, NQ * ZL, LANES), BF), V((4, CH, LANES), F32),
        V((rows, LANES), F32), V((vrows, LANES), F32),
        V((ZL * NP, LANES), F32),
        V((max(modes * LANES, rows), LANES), F32),
        V((2, 2, modes, CH * CH), BF),
        V((YL, CH, ZL * NP), BF), V((YL, CH, ZL * NP), BF), V((CH, HID), BF), V((CH, HID), BF),
        *[V(t.shape, BF) for t in tables],
        pltpu.SemaphoreType.DMA((22,)),
        pltpu.SemaphoreType.DMA((22,)),
        pltpu.SemaphoreType.DMA((2, NQ)),
        pltpu.SemaphoreType.DMA((10,)),
        pltpu.SemaphoreType.DMA((NP,)),
    ]
    state, cotangent = (jnp.transpose(v, (1, 0, 2)) for v in (state, cotangent))
    shape = lambda like: V(like.shape, BF)
    spec = V((2, NQ, CH, LANES), BF)
    grad, grad_sy, grad_sz, grad_in, grad_out = pl.pallas_call(
        functools.partial(kernel, NP, NQ),
        out_shape=(shape(state), spec, spec, shape(w_in), shape(w_in)),
        in_specs=[pl.BlockSpec(memory_space=pl.ANY)] * (6 + len(tables)),
        out_specs=(vmem,) * 5,
        scratch_shapes=scratch,
        compiler_params=pltpu.CompilerParams(
            collective_id=0, has_side_effects=True, vmem_limit_bytes=56 * 1024 * 1024
        ),
    )(state, cotangent, spectral_y, spectral_z, w_in, w_out.T, *[jnp.asarray(t) for t in tables])
    grad_sy, grad_sz = (v.reshape(2, modes, CH * CH) for v in (grad_sy, grad_sz))
    return (jnp.transpose(grad, (1, 0, 2)), grad_sy, grad_sz, grad_in, grad_out.T)


def solution(mesh):
    sizes = (mesh.shape["py"], mesh.shape["pz"])
    in_specs = (P(None, "py", "pz"), P(None, "py", "pz"), P(), P(), P(), P())
    out_specs = (P(None, "py", "pz"), P(), P(), P(), P())
    return jax.shard_map(
        functools.partial(on_device, *sizes),
        mesh=mesh,
        in_specs=in_specs,
        out_specs=out_specs,
        check_vma=False,
    )
```

```python
import functools
import math

import jax
import jax.numpy as jnp
import numpy as np
from jax import lax
from jax.experimental import pallas as pl
from jax.experimental.pallas import tpu as pltpu
from jax.sharding import PartitionSpec as P

MESH = pl.DeviceIdType.MESH
BF, F32 = jnp.bfloat16, jnp.float32
CH, HID = 64, 256
YL, ZL = 6, 8
LANES = 128


def dot_nn(a, b):
    return lax.dot_general(a, b, (((1,), (0,)), ((), ())), preferred_element_type=F32)


def dot_nt(a, b):
    return lax.dot_general(a, b, (((1,), (1,)), ((), ())), preferred_element_type=F32)


def dot_tn(a, b):
    return lax.dot_general(a, b, (((0,), (0,)), ((), ())), preferred_element_type=F32)


def parts_of(value):
    high = value.astype(BF)
    return high, (value - high.astype(F32)).astype(BF)


def np_parts(table):
    high = table.astype(np.float32).astype(BF)
    low = (table - high.astype(np.float64)).astype(np.float32).astype(BF)
    return high, low


def base_tables(length, modes):
    phase = 2.0 * np.pi * (np.outer(np.arange(modes), np.arange(length)) % length) / length
    weight = np.where(np.arange(modes) == 0, 1.0, 2.0)[:, None] / length
    forward = (np.cos(phase), -np.sin(phase))
    inverse = (weight * np.cos(phase), -weight * np.sin(phase))
    return forward, inverse


def y_tables(pair, spans, modes):
    cuts = [table.reshape(modes, spans * 3, 2) for table in pair]
    return np.concatenate([cut[..., odd] for cut in cuts for odd in range(2)], 0)


def swap(value):
    return pltpu.roll(value, 64, 1)


def kernel(
    NP,
    NQ,
    state_in, cot_in, spectral_y, spectral_z, w_in_hbm, w_out_hbm, ytab_hbm, ytabt_hbm, ztab_hbm, ztabt_hbm,
    grad_state, grad_sy, grad_sz, grad_in, grad_out,
    xs, cs, r1, c1, z1, y1s, y1, y2s, y2, z2s, z2, g1, z3, y3s, y3, y4s, y4, z4s, z4, o1, f1,
    us, ur, gs, gr, ws, wr, wg, parts, m1s, m1r, m2r, m3r,
    wi2, wo2, my, mz, pre, gact, actb, gpb, mixb, cotb, uz, gz, vz, su, sg, dws,
    cells_f, spec_f, turn_f, big_f,
    weights_f, state, cotangent, w_in, w_out, ytab, ytabt, ztab, ztabt,
    send_sem, recv_sem, ring_sem, fetch_sem, state_sem,
):
    modes = 2 * NQ
    rows = NP * 24
    vrows = modes * ZL
    share = 256 // NP
    half = NP // 2
    p, q = lax.axis_index("py"), lax.axis_index("pz")
    sibling = q + 1 - 2 * lax.rem(q, 2)

    barrier = pltpu.get_barrier_semaphore()

    first = pltpu.make_async_copy(state_in, state, fetch_sem.at[0])
    first.start()

    @pl.loop(0, half)
    def _(i):
        far = half // 2 + (1 - 2 * lax.rem(i, 2)) * ((i + 1) // 2)
        step = lax.rem(p + far + half, half)
        for side in (1, 0):
            t = step + lax.rem(p // half + side, 2) * half

            @pl.when(t != p)
            def _():
                pl.semaphore_signal(barrier, inc=1, device_id=(t, q), device_id_type=MESH)

    @pl.loop(1, NQ)
    def _(i):
        pl.semaphore_signal(barrier, inc=1, device_id=(p, lax.rem(q + i, NQ)), device_id_type=MESH)

    lo = lax.broadcasted_iota(jnp.int32, (1, LANES), 1) < 64
    pending = []

    def send(kind, slot, source, landing, n, span=(0, half), each=None):
        def start(t, mine, device):
            pltpu.make_async_remote_copy(
                src_ref=source(t),
                dst_ref=landing.at[mine],
                send_sem=send_sem.at[slot],
                recv_sem=recv_sem.at[slot] if each is None else each.at[mine],
                device_id=device,
                device_id_type=MESH,
            ).start()

        if kind == "pz":

            @pl.loop(1, n)
            def _(i):
                t = lax.rem(q + i, n)
                start(t, q, (p, t))

        else:

            @pl.loop(*span)
            def _(i):
                far = half // 2 + (1 - 2 * lax.rem(i, 2)) * ((i + 1) // 2)
                step = lax.rem(p + far + half, half)
                sides = (0, 1) if kind == "py" else (kind,)
                for side in sides:
                    t = step + (lax.rem(p // half + 1 + side, 2) if kind == "py" else side) * half

                    @pl.when(t != p)
                    def _():
                        start(t, p, (t, q))

            if span[1] < half or kind != "py":
                return

        pending.append((slot, landing, n))

    def drain(slot, landing, n):
        span = landing.at[pl.ds(0, n - 1)]
        return pltpu.make_async_remote_copy(
            src_ref=span,
            dst_ref=span,
            send_sem=send_sem.at[slot],
            recv_sem=recv_sem.at[slot],
            device_id=(p, q),
            device_id_type=MESH,
        )

    def arrived(slot, landing, n):
        drain(slot, landing, n).wait_recv()

    def own(landing, at, value):
        landing[pl.ds(at, 1)] = value

    def to_blocks(source, blocks):
        for j in range(3):
            turn_f[...] = jnp.concatenate([source[2 * j], source[2 * j + 1]], 0).astype(F32).T
            for x in range(NP):
                big_f[pl.ds(x * 24 + j * ZL, ZL), :] = turn_f[pl.ds(x, ZL, stride=NP), :]
        blocks[...] = big_f[:rows, :].reshape(NP, 24, LANES).astype(BF)

    def from_blocks(blocks, target):
        big_f[:rows, :] = blocks[...].astype(F32).reshape(rows, LANES)
        for j in range(3):
            cells = [big_f[pl.ds(j * ZL + z, NP, stride=24), :] for z in range(ZL)]
            turned = jnp.concatenate(cells, 0).T.astype(BF)
            target[2 * j] = turned[:64]
            target[2 * j + 1] = turned[64:]

    def mixing(weights):
        @pl.loop(0, 8)
        def _(step):
            for n in range(4):
                g = step * 4 + n
                at = pl.ds(pl.multiple_of(g * LANES, LANES), LANES)
                re, im = weights[0, :, at].astype(F32), weights[1, :, at].astype(F32)
                re_s, im_s = swap(re), swap(im)
                big_f[pl.ds(2 * g, modes, stride=LANES), :] = jnp.where(lo, re, im_s)
                big_f[pl.ds(2 * g + 1, modes, stride=LANES), :] = jnp.where(lo, re_s, im)
                big_f[pl.ds(64 + 2 * g, modes, stride=LANES), :] = jnp.where(lo, -im, re_s)
                big_f[pl.ds(65 + 2 * g, modes, stride=LANES), :] = jnp.where(lo, -im_s, re)

    fetches = [
        pltpu.make_async_copy(source, target, fetch_sem.at[n])
        for n, (source, target) in enumerate(
            [
                (state_in, state), (cot_in, cotangent),
                (spectral_z, weights_f.at[0]), (spectral_y, weights_f.at[1]),
                (w_in_hbm, w_in), (w_out_hbm, w_out),
                (ytab_hbm, ytab), (ytabt_hbm, ytabt), (ztab_hbm, ztab), (ztabt_hbm, ztabt),
            ]
        )
    ]
    for fetch in fetches[1:]:
        fetch.start()
    first.wait()
    to_blocks(state, xs)
    pl.semaphore_wait(barrier, NP - 1 + NQ - 1)

    send("py", 0, lambda t: xs.at[t], r1, NP, each=state_sem)
    own(r1, p, xs[pl.ds(p, 1)])
    fetches[1].wait()
    to_blocks(cotangent, cs)
    for fetch in fetches[2:]:
        fetch.wait()
    mixing(weights_f.at[0])

    @pl.loop(0, modes)
    def _(k):
        mz[k] = big_f[pl.ds(pl.multiple_of(k * LANES, LANES), LANES), :].astype(BF)

    mixing(weights_f.at[1])
    for j in range(2):
        my[j] = big_f[pl.ds(pl.multiple_of((2 * q + j) * LANES, LANES), LANES), :].astype(BF)
    wi2[...] = jnp.zeros_like(wi2)
    wo2[...] = jnp.zeros_like(wo2)
    for j in range(2):
        wi2[j * 64:(j + 1) * 64, j * HID:(j + 1) * HID] = w_in[...]
        wo2[j * 64:(j + 1) * 64, j * HID:(j + 1) * HID] = w_out[...]
    uz[...] = jnp.zeros_like(uz)
    gz[...] = jnp.zeros_like(gz)
    def lines(block):
        return block.astype(F32).reshape(rows, LANES)

    def y_analysis(table, field, sends):
        cells_f[...] = lines(field[...])
        for pair in range(ZL // 2):
            two = [cells_f[pl.ds(2 * pair + i, 3 * NP, stride=ZL), :] for i in range(2)]
            both = jnp.concatenate(two, 1).astype(BF)
            spec = dot_nn(table[...], jnp.concatenate([both, both], 0))
            for i in range(2):
                a, b, c, d = (
                    spec[n * modes:(n + 1) * modes, i * LANES:(i + 1) * LANES] for n in range(4)
                )
                spec_f[pl.ds(2 * pair + i, modes, stride=ZL), :] = jnp.where(
                    lo, a + swap(b), swap(c) + d
                )
        sends[...] = spec_f[...].reshape(NQ, 2 * ZL, LANES).astype(BF)

    def y_synthesis(table, spec):
        spec_f[...] = spec[...].astype(F32).reshape(vrows, LANES)
        for pair in range(ZL // 2):
            two = []
            for i in range(2):
                value = spec_f[pl.ds(2 * pair + i, modes, stride=ZL), :]
                other = swap(value)
                two.append(
                    jnp.concatenate(
                        [
                            jnp.where(lo, value, 0.0), jnp.where(lo, 0.0, other),
                            jnp.where(lo, other, 0.0), jnp.where(lo, 0.0, value),
                        ],
                        0,
                    )
                )
            both = jnp.concatenate(two, 1).astype(BF)
            cells = dot_nn(table[...], jnp.concatenate([both, both], 0))
            for i in range(2):
                cells_f[pl.ds(2 * pair + i, 3 * NP, stride=ZL), :] = cells[
                    :, i * LANES:(i + 1) * LANES
                ]

    def z_analysis(table, landing, store):
        both = table[...]
        for h in range(2):
            block = landing[:, h].astype(F32)
            for j in range(3):
                cells = block[:, j * ZL:(j + 1) * ZL].reshape(NQ * ZL, LANES).astype(BF)
                spec = dot_nn(both, jnp.concatenate([cells, cells], 0))
                re, im = spec[:modes], spec[modes:]
                at = (h * 3 + j) * 2 * modes
                store[pl.ds(at, modes), :] = jnp.where(lo, re, swap(im))
                store[pl.ds(at + modes, modes), :] = jnp.where(lo, swap(re), im)

    def z_synthesis(table, source, sends):
        three = table[...]
        for h in range(2):
            out = []
            for j in range(3):
                at = (h * 3 + j) * 2 * modes
                even, odd = source[pl.ds(at, modes), :], source[pl.ds(at + modes, modes), :]
                spec = jnp.concatenate(
                    [jnp.where(lo, even, swap(odd)), jnp.where(lo, swap(even), odd)], 0
                )
                sh, sl = parts_of(spec)
                cells = dot_nn(three, jnp.concatenate([sh, sl, sh], 0))
                out.append(cells.reshape(NQ, ZL, LANES))
            sends[:, h] = jnp.concatenate(out, 1).astype(BF)

    unroll = min(8, modes)

    def z_split(source, sends):
        @pl.loop(0, modes // unroll)
        def _(step):
            for j in range(unroll):
                k = step * unroll + j
                sends[k] = source[pl.ds(k, 16, stride=modes), :].astype(BF)

    def z_mix(source, store, transposed):
        @pl.loop(0, modes // unroll)
        def _(step):
            for j in range(unroll):
                k = step * unroll + j
                high, low = parts_of(source[pl.ds(k, 16, stride=modes), :])
                both = jnp.concatenate([high, low], 0)
                got = dot_nt(both, mz[k]) if transposed else dot_nn(both, mz[k])
                store[pl.ds(k, 16, stride=modes), :] = got[:16] + got[16:]

    def fold(outer):
        top, bottom = outer[:64], swap(outer[64:])
        return top + jnp.where(lo, bottom, -bottom)

    second = (lax.broadcasted_iota(jnp.int32, (vrows, 1), 0) // ZL) % 2 == 1

    def y_mix(landing, dot):
        value = landing[...].reshape(vrows, LANES)
        return jnp.where(second, dot(value, my[1]), dot(value, my[0])).astype(BF).reshape(
            NQ, 2 * ZL, LANES
        )

    quarter = NQ // 2

    @pl.loop(0, quarter)
    def _(i):
        far = quarter // 2 + (1 - 2 * lax.rem(i, 2)) * ((i + 1) // 2)
        step = lax.rem(lax.rem(p, half) // 2 + far + quarter, quarter)
        for side in (0, 1):
            t = step + lax.rem(p // half + 1 + side, 2) * quarter
            for n in range(2):
                block = 2 * t + n

                @pl.when(block != p)
                def _():
                    at = r1.at[block]
                    pltpu.make_async_remote_copy(
                        src_ref=at,
                        dst_ref=at,
                        send_sem=send_sem.at[0],
                        recv_sem=state_sem.at[block],
                        device_id=(p, q),
                        device_id_type=MESH,
                    ).wait_recv()

            @pl.when(t != q)
            def _():
                pltpu.make_async_remote_copy(
                    src_ref=r1.at[pl.ds(2 * t, 2)],
                    dst_ref=z1.at[q],
                    send_sem=send_sem.at[1],
                    recv_sem=recv_sem.at[1],
                    device_id=(p, t),
                    device_id_type=MESH,
                ).start()

    pending.append((1, z1, NQ))
    own(z1, q, r1[pl.ds(2 * q, 2)].reshape(1, 2, 24, LANES))
    y_analysis(ytab.at[0], r1, y1s)
    send("pz", 3, lambda t: y1s.at[t], y1, NQ)
    send("py", 2, lambda t: cs.at[t], c1, NP)
    own(c1, p, cs[pl.ds(p, 1)])
    own(y1, q, y1s[pl.ds(q, 1)])
    arrived(1, z1, NQ)
    z_analysis(ztab.at[0], z1, uz)
    z_mix(uz, vz, False)
    z_synthesis(ztabt.at[1], vz, z2s)
    send("pz", 5, lambda t: z2s.at[t], z2, NQ)
    own(z2, q, z2s[pl.ds(q, 1)])
    arrived(3, y1, NQ)
    y2s[...] = y_mix(y1, dot_nn)
    send("pz", 4, lambda t: y2s.at[t], y2, NQ)
    own(y2, q, y2s[pl.ds(q, 1)])
    z_split(uz, us)
    send("pz", 17, lambda t: us.at[pl.ds(2 * t, 2)], ur, NQ)
    own(ur, q, us[pl.ds(2 * q, 2)].reshape(1, 2, 16, LANES))
    arrived(4, y2, NQ)
    y_synthesis(ytabt.at[1], y2)
    arrived(5, z2, NQ)
    mixb[...] = (cells_f[...].astype(BF).astype(F32) + lines(z2[...])).astype(BF)

    arrived(2, c1, NP)
    cotb[...] = lines(c1[...]).astype(BF)
    chunks = min(4, NQ)
    per = rows // chunks
    tile = 32 if per % 32 == 0 else 16
    root = math.sqrt(2.0 / math.pi)

    @pl.loop(0, chunks)
    def _(turn):
        chunk = lax.rem(turn + 1 + q // (NQ // chunks), chunks)
        start = pl.multiple_of(chunk * per, per)
        pre[...] = dot_nn(mixb[pl.ds(start, per), :], wi2[...])
        gact[...] = dot_nn(cotb[pl.ds(start, per), :], wo2[...])

        @pl.loop(0, per // tile)
        def _(step):
            here = pl.ds(pl.multiple_of(step * tile, tile), tile)
            at = pl.ds(pl.multiple_of(start + step * tile, tile), tile)
            value = pre[here, :]
            square = value * value
            bend = jnp.tanh(value * (root + (root * 0.044715) * square))
            rise = 0.5 + 0.5 * bend
            slope = rise + (0.5 * value) * (1.0 - bend * bend) * (
                root + (3.0 * root * 0.044715) * square
            )
            actb[at, :] = (value * rise).astype(BF)
            gpb[at, :] = (gact[here, :] * slope).astype(BF)

        back = dot_nt(gpb[pl.ds(start, per), :], wi2[...])
        g1[pl.ds(chunk * (NP // chunks), NP // chunks)] = back.reshape(
            NP // chunks, 24, LANES
        ).astype(BF)

        @pl.loop(0, NQ // chunks)
        def _(n):
            t = chunk * (NQ // chunks) + n

            @pl.when(t != q)
            def _():
                pltpu.make_async_remote_copy(
                    src_ref=g1.at[pl.ds(2 * t, 2)],
                    dst_ref=z3.at[q],
                    send_sem=send_sem.at[6],
                    recv_sem=recv_sem.at[6],
                    device_id=(p, t),
                    device_id_type=MESH,
                ).start()

    pending.append((6, z3, NQ))
    own(z3, q, g1[pl.ds(2 * q, 2)].reshape(1, 2, 24, LANES))
    y_analysis(ytab.at[1], g1, y3s)
    send("pz", 7, lambda t: y3s.at[t], y3, NQ)
    own(y3, q, y3s[pl.ds(q, 1)])

    def diagonal(both):
        return both[:64, :HID] + both[64:, HID:]

    dwi = diagonal(dot_tn(mixb[...], gpb[...]))
    dwo = diagonal(dot_tn(cotb[...], actb[...]))
    m1s[...] = jnp.concatenate(
        [dwi[:, :LANES], dwi[:, LANES:], dwo[:, :LANES], dwo[:, LANES:]], 0
    ).reshape(NP, share, LANES).astype(BF)
    send("py", 8, lambda t: m1s.at[t], m1r, NP)
    own(m1r, p, m1s[pl.ds(p, 1)])

    arrived(6, z3, NQ)
    z_analysis(ztab.at[1], z3, gz)
    z_split(gz, gs)
    send("pz", 10, lambda t: gs.at[pl.ds(2 * t, 2)], gr, NQ)
    own(gr, q, gs[pl.ds(2 * q, 2)].reshape(1, 2, 16, LANES))
    arrived(7, y3, NQ)
    y4s[...] = y_mix(y3, dot_nt)
    send("pz", 9, lambda t: y4s.at[t], y4, NQ)
    own(y4, q, y4s[pl.ds(q, 1)])

    for landing, store in ((y1, su), (y3, sg)):
        value = landing[...].astype(F32)
        for j in range(2):
            at = value[:, j * ZL:(j + 1) * ZL]
            store[j] = at.reshape(NQ * ZL, LANES).astype(BF)

    @pl.loop(0, 2)
    def _(j):
        dws[j] = fold(dot_tn(su[j], sg[j]))

    def scatter(branch, slot):
        out = [[], []]
        for j in range(2):
            even, odd = (dws[2 * branch + j, pl.ds(n, 32, stride=2), :] for n in range(2))
            out[0].append(jnp.where(lo, even, swap(odd)))
            out[1].append(jnp.where(lo, swap(even), odd))
        ws[branch] = jnp.concatenate(out[0] + out[1], 0).reshape(half, share, LANES).astype(BF)
        send(branch, slot, lambda t: ws.at[branch, t - branch * half], wr, NP)

        @pl.when(p // half == branch)
        def _():
            own(wr, p, ws[branch, pl.ds(p - branch * half, 1)])

    def gather(branch, slot, into, scale):
        @pl.when(p // half == branch)
        def _():
            arrived(slot, wr, NP)
            wg[...] = (jnp.sum(wr[...].astype(F32), axis=0) * scale).astype(BF)
            own(parts.at[branch], p - branch * half, wg[...].reshape(1, share, LANES))

            @pl.loop(0, half)
            def _(i):
                far = half // 2 + (1 - 2 * lax.rem(i, 2)) * ((i + 1) // 2)
                step = lax.rem(p + far + half, half)
                for side in (0, 1):
                    t = step + lax.rem(branch + 1 + side, 2) * half

                    @pl.when(t != p)
                    def _():
                        pltpu.make_async_remote_copy(
                            src_ref=wg,
                            dst_ref=parts.at[branch, p - branch * half],
                            send_sem=send_sem.at[into],
                            recv_sem=recv_sem.at[into],
                            device_id=(t, q),
                            device_id_type=MESH,
                        ).start()

    def settle(branch, slot, into):
        @pl.when(p // half == branch)
        def _():
            drain(slot, ws.at[branch], half).wait_send()
            drain(into, wr, NP).wait_send()

        @pl.when(p // half != branch)
        def _():
            drain(slot, ws.at[branch], half + 1).wait_send()

    scatter(0, 13)
    z_mix(gz, vz, True)
    z_synthesis(ztabt.at[0], vz, z4s)
    send("pz", 11, lambda t: z4s.at[t], z4, NQ)
    own(z4, q, z4s[pl.ds(q, 1)])
    arrived(17, ur, NQ)
    arrived(10, gr, NQ)

    @pl.loop(0, 2)
    def _(j):
        dws[2 + j] = fold(
            dot_tn(ur[:, j].reshape(NQ * 16, LANES), gr[:, j].reshape(NQ * 16, LANES))
        )

    scatter(1, 15)
    arrived(8, m1r, NP)
    own(m2r, q, jnp.sum(m1r[...].astype(F32), axis=0, keepdims=True))
    send("pz", 14, lambda t: m2r.at[q], m2r, NQ)

    arrived(9, y4, NQ)
    y_synthesis(ytabt.at[0], y4)
    arrived(11, z4, NQ)
    total = lines(c1[...]) + cells_f[...].astype(BF).astype(F32) + lines(z4[...])
    o1[...] = total.reshape(NP, 24, LANES).astype(BF)
    scale_y = 1.0 / math.sqrt(NP * ZL * NQ)
    scale_z = 1.0 / math.sqrt(NP * YL * NP)
    scale_mlp = 1.0 / math.sqrt(NP * (YL * NP) * (ZL * NQ))
    gather(0, 13, 16, scale_y)
    send("py", 12, lambda t: o1.at[t], f1, NP, (0, half // 4))
    own(f1, p, o1[pl.ds(p, 1)])
    gather(1, 15, 18, scale_z)
    send("py", 12, lambda t: o1.at[t], f1, NP, (half // 4, half))
    arrived(14, m2r, NQ)
    own(m3r, p, (jnp.sum(m2r[...], axis=0, keepdims=True) * scale_mlp).astype(BF))
    send("py", 19, lambda t: m3r.at[p], m3r, NP)

    targets = (grad_sy, grad_sz)

    def ring(branch, slot, device):
        at = targets[branch].at[:, slot]
        return pltpu.make_async_remote_copy(
            src_ref=at,
            dst_ref=at,
            send_sem=send_sem.at[20 + branch],
            recv_sem=ring_sem.at[branch, slot],
            device_id=(p, device),
            device_id_type=MESH,
        )

    def ring_start(branch, into):
        @pl.when(p // half == branch)
        def _():
            drain(into, parts.at[branch], half).wait_recv()

        @pl.when(p // half != branch)
        def _():
            drain(into, parts.at[branch], half + 1).wait_recv()

        whole = parts[branch].astype(F32).reshape(2, 1, CH, LANES).astype(BF)
        targets[branch][:, pl.ds(q, 1)] = whole

        @pl.loop(1, NQ // 2)
        def _(j):
            ring(branch, q, lax.rem(q + 2 * j, NQ)).start()

        ring(branch, q, sibling).start()

    def ring_pass(branch):
        @pl.loop(1, NQ // 2)
        def _(j):
            slot = lax.rem(q + 2 * j, NQ)
            ring(branch, slot, sibling).wait_recv()
            ring(branch, slot, sibling).start()

    def ring_end(branch):
        @pl.loop(0, NQ // 2)
        def _(j):
            ring(branch, lax.rem(sibling + 2 * j, NQ), sibling).wait_recv()

    ring_start(0, 16)
    ring_start(1, 18)
    ring_pass(0)
    ring_pass(1)
    arrived(12, f1, NP)
    from_blocks(f1, grad_state)
    arrived(19, m3r, NP)
    small = m3r[...].reshape(256, LANES)
    grad_in[...] = jnp.concatenate([small[:64], small[64:128]], 1)
    grad_out[...] = jnp.concatenate([small[128:192], small[192:]], 1)
    ring_end(0)
    ring_end(1)

    for item in pending:
        drain(*item).wait_send()
    settle(0, 13, 16)
    settle(1, 15, 18)
    for branch in range(2):
        span = targets[branch].at[:, pl.ds(0, NQ - 1)]
        pltpu.make_async_remote_copy(
            src_ref=span,
            dst_ref=span,
            send_sem=send_sem.at[20 + branch],
            recv_sem=ring_sem.at[branch, 0],
            device_id=(p, q),
            device_id_type=MESH,
        ).wait_send()


def on_device(NP, NQ, state, cotangent, spectral_y, spectral_z, w_in, w_out):
    modes = 2 * NQ
    rows = NP * 24
    vrows = modes * ZL
    share = 256 // NP

    forward_y, inverse_y = base_tables(YL * NP, modes)
    forward_z, inverse_z = base_tables(ZL * NQ, modes)
    yf = np_parts(y_tables(forward_y, NP, modes))
    ya = np_parts(y_tables(inverse_y, NP, modes))
    zf = np_parts(np.concatenate(forward_z, 0))
    za = np_parts(np.concatenate(inverse_z, 0))
    flip = lambda pair: [v.T for v in pair]
    tables = [
        np.stack([np.concatenate(v, 1) for v in (yf, ya)]),
        np.stack([np.concatenate(flip(v), 1) for v in (yf, ya)]),
        np.stack([np.concatenate(v, 1) for v in (zf, za)]),
        np.stack([np.concatenate([v[0].T, v[0].T, v[1].T], 1) for v in (zf, za)]),
    ]

    vmem = pl.BlockSpec(memory_space=pltpu.VMEM)
    V = pltpu.VMEM
    field = lambda: V((NP, 24, LANES), BF)
    zbuf = lambda: V((NQ, 2, 24, LANES), BF)
    ybuf = lambda: V((NQ, 2 * ZL, LANES), BF)
    pack = lambda kind: V((NP, share, LANES), kind)
    scratch = [
        field(), field(), field(), field(), zbuf(), ybuf(), ybuf(), ybuf(), ybuf(), zbuf(), zbuf(),
        field(), zbuf(), ybuf(), ybuf(), ybuf(), ybuf(), zbuf(), zbuf(), field(), field(),
        V((modes, 16, LANES), BF), V((NQ, 2, 16, LANES), BF),
        V((modes, 16, LANES), BF), V((NQ, 2, 16, LANES), BF),
        V((2, NP // 2, share, LANES), BF), pack(BF), V((share, LANES), BF),
        V((2, NP // 2, share, LANES), BF),
        pack(BF), pack(BF), V((NQ, share, LANES), F32), pack(BF),
        V((LANES, 2 * HID), BF), V((LANES, 2 * HID), BF),
        V((2, LANES, LANES), BF), V((modes, LANES, LANES), BF),
        V((rows // min(4, NQ), 2 * HID), F32), V((rows // min(4, NQ), 2 * HID), F32),
        V((rows, 2 * HID), BF), V((rows, 2 * HID), BF), V((rows, LANES), BF), V((rows, LANES), BF),
        V((16 * modes, LANES), F32), V((16 * modes, LANES), F32), V((16 * modes, LANES), F32),
        V((2, NQ * ZL, LANES), BF), V((2, NQ * ZL, LANES), BF), V((4, CH, LANES), F32),
        V((rows, LANES), F32), V((vrows, LANES), F32),
        V((ZL * NP, LANES), F32),
        V((max(modes * LANES, rows), LANES), F32),
        V((2, 2, modes, CH * CH), BF),
        V((YL, CH, ZL * NP), BF), V((YL, CH, ZL * NP), BF), V((CH, HID), BF), V((CH, HID), BF),
        *[V(t.shape, BF) for t in tables],
        pltpu.SemaphoreType.DMA((22,)),
        pltpu.SemaphoreType.DMA((22,)),
        pltpu.SemaphoreType.DMA((2, NQ)),
        pltpu.SemaphoreType.DMA((10,)),
        pltpu.SemaphoreType.DMA((NP,)),
    ]
    state, cotangent = (jnp.transpose(v, (1, 0, 2)) for v in (state, cotangent))
    shape = lambda like: V(like.shape, BF)
    spec = V((2, NQ, CH, LANES), BF)
    grad, grad_sy, grad_sz, grad_in, grad_out = pl.pallas_call(
        functools.partial(kernel, NP, NQ),
        out_shape=(shape(state), spec, spec, shape(w_in), shape(w_in)),
        in_specs=[pl.BlockSpec(memory_space=pl.ANY)] * (6 + len(tables)),
        out_specs=(vmem,) * 5,
        scratch_shapes=scratch,
        compiler_params=pltpu.CompilerParams(
            collective_id=0, has_side_effects=True, vmem_limit_bytes=56 * 1024 * 1024
        ),
    )(state, cotangent, spectral_y, spectral_z, w_in, w_out.T, *[jnp.asarray(t) for t in tables])
    grad_sy, grad_sz = (v.reshape(2, modes, CH * CH) for v in (grad_sy, grad_sz))
    return (jnp.transpose(grad, (1, 0, 2)), grad_sy, grad_sz, grad_in, grad_out.T)


def solution(mesh):
    sizes = (mesh.shape["py"], mesh.shape["pz"])
    in_specs = (P(None, "py", "pz"), P(None, "py", "pz"), P(), P(), P(), P())
    out_specs = (P(None, "py", "pz"), P(), P(), P(), P())
    return jax.shard_map(
        functools.partial(on_device, *sizes),
        mesh=mesh,
        in_specs=in_specs,
        out_specs=out_specs,
        check_vma=False,
    )
```
